32 devices in a mesh: row: 16 (over z, y, core), col: 2 (over x).
Axes of the slice: x: 2, y: 2, z: 4, core: 2. Of those that a mesh axis runs over, the one named last changes fastest.
Arguments:
- vectors: float32 [32, 65536], P(None, ('row', 'col')), may hold values from -6 to 6
- block_values: bfloat16 [8192, 128, 128], P(('row', 'col')), may hold values from -0.15625 to 0.15625
- block_rows: int32 [8192], P(('row', 'col')), may hold values from 0 to 31, as said below
- block_cols: int32 [8192], P(('row', 'col')), may hold values from 0 to 255, as said below
- block_counts: int32 [32], P(('row', 'col')), may hold values from 32 to 256, as said below
- center: float32 [1], replicated, may hold values from -0.5 to 0.5
- radius: float32 [1], replicated, may hold values from 1.5 to 3
Outputs:
- filtered: float32 [32, 65536], P(None, ('row', 'col'))
The draws below stay inside these ranges and needn't reach their ends.
Inputs may be any that keep to these rules, and one draw needn't show every extreme that they name: `block_counts`: live slots of each device; some device fills all 256 slots. `block_rows`: Block-row inside the row group; slots may repeat a position. `block_cols`: Block-column inside the col group; slots may repeat a position.
All inputs are finite; a program needn't handle non-finite values.
Results may differ from the reference program's by a relative error of at most 0.02.
Values may be sent and summed in bfloat16 or wider, within the bound.
No kernel may reach another device: no remote copies, remote signals or barrier semaphores. Data moves between devices by JAX's collectives and lax.ppermute only.
A program may use at most 128 MiB of HBM per device.

```python
import jax
import jax.numpy as jnp
from jax import lax

K = 32
BS = 128
ROWS_DEV = 2048
CAP = 256
STEPS = 2
N = 65536
BLK_ROWS = 32
BLK_COLS = 256
SLOTS = 8192
N_ROW = 16
N_COL = 2


def draw_block_counts(key, part):
    device_total = SLOTS // CAP
    drawn_values = jax.random.randint(jax.random.fold_in(key, 11), (device_total,), 0, CAP + 1)
    counts_all = jnp.maximum(max(CAP // 8, 1), drawn_values * drawn_values // CAP)
    busiest = jax.random.randint(jax.random.fold_in(key, 12), (), 0, device_total)
    counts_all = counts_all.at[busiest].set(CAP)
    counts_all = counts_all.at[(busiest + 1) % device_total].set(max(CAP // 8, 1))
    return counts_all.astype(jnp.int32)


def draw_block_rows(key, part):
    picked = jax.random.randint(jax.random.fold_in(key, 21), (SLOTS,), 0, BLK_ROWS)
    picked = picked.at[0].set(0).at[1].set(BLK_ROWS - 1)
    return picked.astype(jnp.int32)


def draw_block_cols(key, part):
    picked = jax.random.randint(jax.random.fold_in(key, 31), (SLOTS,), 0, BLK_COLS)
    picked = picked.at[0].set(0).at[1].set(BLK_COLS - 1)
    return picked.astype(jnp.int32)


def block_scale(key, dims, split, least, largest):
    factor_of = 1.0
    for dim, blocks in split:
        draws = jax.random.uniform(jax.random.fold_in(jax.random.fold_in(key, 6), dim), (blocks,), jnp.float32, least / len(split), largest / len(split))
        factor_of = factor_of * jnp.repeat(jnp.exp(draws), dims[dim] // blocks).reshape((-1,) + (1,) * (len(dims) - 1 - dim))
    return factor_of


def normal_values(stream_key, dims, width, bound, cuts=(), held_as=jnp.bfloat16):
    level = block_scale(stream_key, dims, cuts, -0.22, 0.18) if cuts else 1.0
    result = jax.random.normal(stream_key, dims, jnp.float32) * width * level
    return jnp.minimum(jnp.maximum(result, -bound), bound).astype(held_as)


def setup_inputs(seed: int = 0) -> dict:
    keys = jax.random.split(jax.random.key(seed), 8)
    return {
        "vectors": normal_values(keys[0], (K, N), 1.0, 6.0, ((1, 32),), jnp.float32),
        "block_values": normal_values(keys[1], (SLOTS, BS, BS), (2 * CAP * BS * BS // (3 * ROWS_DEV)) ** -0.5, 0.15625, ((0, 32),)),
        "block_rows": draw_block_rows(jax.random.fold_in(keys[7], 71), 0),
        "block_cols": draw_block_cols(jax.random.fold_in(keys[7], 71), 0),
        "block_counts": draw_block_counts(jax.random.fold_in(keys[7], 71), 0),
        "center": jnp.clip(jax.random.uniform(keys[5], (1,), jnp.float32, -0.5, 0.5), -0.5, 0.5),
        "radius": jnp.clip(jax.random.uniform(keys[6], (1,), jnp.float32, 1.5, 3.0), 1.5, 3.0),
    }


def rounded(values):
    return lax.optimization_barrier(values.astype(jnp.bfloat16)).astype(jnp.float32)


def reference(vectors, block_values, block_rows, block_cols, block_counts, center, radius):
    center_value = center[0]
    radius_value = radius[0]

    def apply_operator(current):
        narrow = current.astype(jnp.bfloat16).reshape(K, N_ROW, N_COL, ROWS_DEV)

        def device_term(device_index, image_sum):
            row_index = device_index // N_COL
            col_index = device_index % N_COL
            row_region = lax.dynamic_index_in_dim(narrow, row_index, 1, keepdims=False).reshape(K, BLK_ROWS, BS).astype(jnp.float32)
            col_region = lax.dynamic_index_in_dim(narrow, col_index, 2, keepdims=False).reshape(K, BLK_COLS, BS).astype(jnp.float32)
            first_slot = (device_index * CAP).astype(jnp.int32)
            blocks = lax.dynamic_slice_in_dim(block_values, first_slot, CAP, 0).astype(jnp.float32)
            rows_here = lax.dynamic_slice_in_dim(block_rows, first_slot, CAP, 0).astype(jnp.int32)
            cols_here = lax.dynamic_slice_in_dim(block_cols, first_slot, CAP, 0).astype(jnp.int32)
            live_slots = (jnp.arange(CAP, dtype=jnp.int32) < block_counts[device_index]).astype(jnp.float32)[:, None, None]
            forward = jnp.einsum("sij,ksj->ski", blocks, jnp.take(col_region, cols_here, axis=1)) * live_slots
            forward = jax.ops.segment_sum(forward, rows_here, num_segments=BLK_ROWS)
            mirror = jnp.einsum("sij,ksi->skj", blocks, jnp.take(row_region, rows_here, axis=1)) * live_slots
            mirror = jax.ops.segment_sum(mirror, cols_here, num_segments=BLK_COLS)
            forward = rounded(jnp.transpose(forward, (1, 0, 2)).reshape(K, N_COL, ROWS_DEV))
            mirror = rounded(jnp.transpose(mirror, (1, 0, 2)).reshape(K, N_ROW, ROWS_DEV))
            image_sum = image_sum.at[:, row_index].add(forward)
            image_sum = image_sum.at[:, :, col_index].add(mirror)
            return image_sum

        start_image = jnp.zeros((K, N_ROW, N_COL, ROWS_DEV), jnp.float32)
        image_sum = lax.fori_loop(0, N_ROW * N_COL, device_term, start_image)
        return image_sum.reshape(K, N)

    previous = vectors
    current = (apply_operator(vectors) - center_value * vectors) / radius_value
    for repeat_index in range(STEPS - 1):
        following = 2.0 * (apply_operator(current) - center_value * current) / radius_value - previous
        previous = current
        current = following
    return current
```

```python
import functools

import jax
import jax.numpy as jnp
from jax import lax
from jax.experimental import pallas as pl
from jax.experimental.pallas import tpu as pltpu
from jax.sharding import PartitionSpec as P

CHUNK = 32
UNROLL = 8


def product_kernel(contract, outputs, n_in, count_ref, take_ref, put_ref, *refs):
    pieces = refs[:n_in]
    blocks = refs[n_in]
    outs = refs[n_in + 1 : n_in + 1 + len(outputs)]
    held, held_blocks, total, piece_sems, block_sems = refs[n_in + 1 + len(outputs) :]
    capacity, size_block = blocks.shape[0], blocks.shape[1]
    per_piece = held.shape[2] // size_block
    chunks = capacity // CHUNK
    count = count_ref[0]

    copies = [pltpu.make_async_copy(pieces[p], held.at[p], piece_sems.at[p]) for p in range(n_in)]
    for copy in copies:
        copy.start()

    def block_copy(g):
        part = pl.ds(g * CHUNK, CHUNK)
        return pltpu.make_async_copy(blocks.at[part], held_blocks.at[part], block_sems.at[g])

    for g in range(chunks):
        @pl.when(g * CHUNK < count)
        def _(g=g):
            block_copy(g).start()

    total[...] = jnp.zeros_like(total)
    for copy in copies:
        copy.wait()

    def group(first):
        places = []
        sums = []
        for n in range(UNROLL):
            slot = first + n
            take = take_ref[slot]
            put = put_ref[slot]
            column = pl.multiple_of((take % per_piece) * size_block, size_block)
            picked = held[take // per_piece, :, pl.ds(column, size_block)]
            sums.append(
                lax.dot_general(
                    picked, held_blocks[slot], (((1,), (contract,)), ((), ())), preferred_element_type=jnp.float32
                )
            )
            column = pl.multiple_of((put % per_piece) * size_block, size_block)
            places.append((put // per_piece, slice(None), pl.ds(column, size_block)))
        for place, value in zip(places, sums):
            total[place] += value

    for g in range(chunks):
        @pl.when(g * CHUNK < count)
        def _(g=g):
            block_copy(g).wait()

            @pl.loop(0, CHUNK // UNROLL)
            def _(n):
                group(g * CHUNK + n * UNROLL)

    for out, held_pieces in zip(outs, outputs):
        for n, p in enumerate(held_pieces):
            out[n] = total[p].astype(out.dtype)


def block_product(contract, outputs, dtypes, n_put, count, take, put, pieces, blocks):
    capacity, size_block = blocks.shape[0], blocks.shape[1]
    vector_count, own_rows = pieces[0].shape
    n_in = len(pieces)
    smem = pl.BlockSpec(memory_space=pltpu.SMEM)
    anywhere = pl.BlockSpec(memory_space=pl.ANY)
    return pl.pallas_call(
        functools.partial(product_kernel, contract, outputs, n_in),
        out_shape=[
            jax.ShapeDtypeStruct((len(held), vector_count, own_rows), dtype) for held, dtype in zip(outputs, dtypes)
        ],
        in_specs=[smem] * 3 + [anywhere] * (n_in + 1),
        out_specs=[pl.BlockSpec(memory_space=pltpu.VMEM)] * len(outputs),
        scratch_shapes=[
            pltpu.VMEM((n_in, vector_count, own_rows), jnp.bfloat16),
            pltpu.VMEM(blocks.shape, blocks.dtype),
            pltpu.VMEM((n_put + 1, vector_count, own_rows), jnp.float32),
            pltpu.SemaphoreType.DMA((n_in,)),
            pltpu.SemaphoreType.DMA((capacity // CHUNK,)),
        ],
        compiler_params=pltpu.CompilerParams(vmem_limit_bytes=40 * 1024 * 1024),
        cost_estimate=pl.CostEstimate(
            flops=2 * capacity * size_block * size_block * 256,
            bytes_accessed=2 * blocks.size + 2 * n_in * vector_count * own_rows,
            transcendentals=0,
        ),
        name="mirror" if contract == 0 else "forward",
    )(count, take, put, *pieces, blocks)


def shards(n_row, n_col, vectors, block_values, block_rows, block_cols, block_counts, center, radius):
    size_block = block_values.shape[1]
    own_rows = vectors.shape[1]
    per_piece = own_rows // size_block
    center_value = center[0]
    radius_value = radius[0]

    n_c = 2 if n_row % 2 == 0 else 1
    n_a = 4 if (n_row // n_c) % 4 == 0 else n_row // n_c
    n_b = n_row // n_c // n_a

    def at(a, b, c):
        return ((a % n_a) * n_b + b % n_b) * n_c + c % n_c

    spots = [(a, b, c) for a in range(n_a) for b in range(n_b) for c in range(n_c)]

    def shift(value, da=0, db=0, dc=0):
        pairs = [(at(a, b, c), at(a + da, b + db, c + dc)) for a, b, c in spots]
        return lax.ppermute(value, "row", pairs)

    def shift_col(value, d):
        return lax.ppermute(value, "col", [(j, (j + d) % n_col) for j in range(n_col)])

    row_index = lax.axis_index("row").astype(jnp.int32)
    col_index = lax.axis_index("col").astype(jnp.int32)
    my_c, my_b, my_a = row_index % n_c, row_index // n_c % n_b, row_index // (n_c * n_b)

    def piece(da, db, dc):
        return (dc * n_b + db) * n_a + da

    owner = block_cols // per_piece
    owner_c, owner_b, owner_a = owner % n_c, owner // n_c % n_b, owner // (n_c * n_b)
    place_cols = (
        piece((my_a - owner_a + n_a) % n_a, (my_b - owner_b + n_b) % n_b, (my_c - owner_c + n_c) % n_c) * per_piece
        + block_cols % per_piece
    )
    place_rows = (col_index - block_rows // per_piece + n_col) % n_col * per_piece + block_rows % per_piece
    live = jnp.arange(block_rows.shape[0], dtype=jnp.int32) < block_counts[0]
    put_cols = jnp.where(live, place_cols, n_row * per_piece)
    put_rows = jnp.where(live, place_rows, n_col * per_piece)

    mirror_outputs = [
        [piece(a, b, c) for a in range(n_a)] for c in range(n_c) for b in range(n_b)
    ]
    forward_outputs = [[j] for j in range(n_col)]

    def apply_operator(narrow):
        by_col = [narrow] + [shift_col(narrow, j) for j in range(1, n_col)]

        along_a = [narrow] + [shift(narrow, da=a) for a in range(1, n_a)]
        along_b = list(along_a)
        for b in range(1, n_b):
            along_b += [shift(part, db=b) for part in along_a]
        by_row = list(along_b)
        for c in range(1, n_c):
            by_row += [shift(part, dc=c) for part in along_b]

        mirrors = block_product(
            0, mirror_outputs, [jnp.bfloat16] * len(mirror_outputs), n_row,
            block_counts, place_rows, put_cols, by_col, block_values,
        )
        by_b = []
        for b in range(n_b):
            share = mirrors[b].astype(jnp.float32)
            for c in range(1, n_c):
                share += shift(mirrors[c * n_b + b], dc=-c).astype(jnp.float32)
            by_b.append(share)
        share = by_b[0]
        for b in range(1, n_b):
            share += shift(by_b[b].astype(jnp.bfloat16), db=-b).astype(jnp.float32)
        mirror_sum = share[0]
        for a in range(1, n_a):
            mirror_sum += shift(share[a].astype(jnp.bfloat16), da=-a).astype(jnp.float32)

        forwards = block_product(
            1, forward_outputs, [jnp.float32] + [jnp.bfloat16] * (n_col - 1), n_col,
            block_counts, place_cols, put_rows, by_row, block_values,
        )
        forward_sum = forwards[0][0]
        for j in range(1, n_col):
            forward_sum += shift_col(forwards[j][0], -j).astype(jnp.float32)
        return forward_sum + mirror_sum

    current = (apply_operator(vectors.astype(jnp.bfloat16)) - center_value * vectors) / radius_value
    return 2.0 * (apply_operator(current.astype(jnp.bfloat16)) - center_value * current) / radius_value - vectors


def solution(mesh):
    return jax.shard_map(
        functools.partial(shards, mesh.shape["row"], mesh.shape["col"]),
        mesh=mesh,
        in_specs=(
            P(None, ("row", "col")),
            P(("row", "col"), None, None),
            P(("row", "col")),
            P(("row", "col")),
            P(("row", "col")),
            P(),
            P(),
        ),
        out_specs=P(None, ("row", "col")),
        check_vma=False,
    )
```

```python
import functools

import jax
import jax.numpy as jnp
from jax import lax
from jax.experimental import pallas as pl
from jax.experimental.pallas import tpu as pltpu
from jax.sharding import PartitionSpec as P

CHUNK = 32
UNROLL = 8


def product_kernel(contract, outputs, n_in, count_ref, take_ref, put_ref, *refs):
    pieces = refs[:n_in]
    blocks = refs[n_in]
    outs = refs[n_in + 1 : n_in + 1 + len(outputs)]
    held, held_blocks, total, piece_sems, block_sems = refs[n_in + 1 + len(outputs) :]
    capacity, size_block = blocks.shape[0], blocks.shape[1]
    per_piece = held.shape[2] // size_block
    chunks = capacity // CHUNK
    count = count_ref[0]

    copies = [pltpu.make_async_copy(pieces[p], held.at[p], piece_sems.at[p]) for p in range(n_in)]
    for copy in copies:
        copy.start()

    def block_copy(g):
        part = pl.ds(g * CHUNK, CHUNK)
        return pltpu.make_async_copy(blocks.at[part], held_blocks.at[part], block_sems.at[g])

    for g in range(chunks):
        @pl.when(g * CHUNK < count)
        def _(g=g):
            block_copy(g).start()

    total[...] = jnp.zeros_like(total)
    for copy in copies:
        copy.wait()

    def group(first):
        places = []
        sums = []
        for n in range(UNROLL):
            slot = first + n
            take = take_ref[slot]
            put = put_ref[slot]
            column = pl.multiple_of((take % per_piece) * size_block, size_block)
            picked = held[take // per_piece, :, pl.ds(column, size_block)]
            sums.append(
                lax.dot_general(
                    picked, held_blocks[slot], (((1,), (contract,)), ((), ())), preferred_element_type=jnp.float32
                )
            )
            column = pl.multiple_of((put % per_piece) * size_block, size_block)
            places.append((put // per_piece, slice(None), pl.ds(column, size_block)))
        for place, value in zip(places, sums):
            total[place] += value

    for g in range(chunks):
        @pl.when(g * CHUNK < count)
        def _(g=g):
            block_copy(g).wait()

            @pl.loop(0, CHUNK // UNROLL)
            def _(n):
                group(g * CHUNK + n * UNROLL)

    for out, held_pieces in zip(outs, outputs):
        for n, p in enumerate(held_pieces):
            out[n] = total[p].astype(out.dtype)


def block_product(contract, outputs, dtypes, n_put, count, take, put, pieces, blocks):
    capacity, size_block = blocks.shape[0], blocks.shape[1]
    vector_count, own_rows = pieces[0].shape
    n_in = len(pieces)
    smem = pl.BlockSpec(memory_space=pltpu.SMEM)
    anywhere = pl.BlockSpec(memory_space=pl.ANY)
    return pl.pallas_call(
        functools.partial(product_kernel, contract, outputs, n_in),
        out_shape=[
            jax.ShapeDtypeStruct((len(held), vector_count, own_rows), dtype) for held, dtype in zip(outputs, dtypes)
        ],
        in_specs=[smem] * 3 + [anywhere] * (n_in + 1),
        out_specs=[pl.BlockSpec(memory_space=pltpu.VMEM)] * len(outputs),
        scratch_shapes=[
            pltpu.VMEM((n_in, vector_count, own_rows), jnp.bfloat16),
            pltpu.VMEM(blocks.shape, blocks.dtype),
            pltpu.VMEM((n_put + 1, vector_count, own_rows), jnp.float32),
            pltpu.SemaphoreType.DMA((n_in,)),
            pltpu.SemaphoreType.DMA((capacity // CHUNK,)),
        ],
        compiler_params=pltpu.CompilerParams(vmem_limit_bytes=40 * 1024 * 1024),
        cost_estimate=pl.CostEstimate(
            flops=2 * capacity * size_block * size_block * 256,
            bytes_accessed=2 * blocks.size + 2 * n_in * vector_count * own_rows,
            transcendentals=0,
        ),
        name="mirror" if contract == 0 else "forward",
    )(count, take, put, *pieces, blocks)


def shards(n_row, n_col, vectors, block_values, block_rows, block_cols, block_counts, center, radius):
    size_block = block_values.shape[1]
    own_rows = vectors.shape[1]
    per_piece = own_rows // size_block
    center_value = center[0]
    radius_value = radius[0]

    n_c = 2 if n_row % 2 == 0 else 1
    n_a = 4 if (n_row // n_c) % 4 == 0 else n_row // n_c
    n_b = n_row // n_c // n_a

    def at(a, b, c):
        return ((a % n_a) * n_b + b % n_b) * n_c + c % n_c

    spots = [(a, b, c) for a in range(n_a) for b in range(n_b) for c in range(n_c)]

    def shift(value, da=0, db=0, dc=0):
        pairs = [(at(a, b, c), at(a + da, b + db, c + dc)) for a, b, c in spots]
        return lax.ppermute(value, "row", pairs)

    def shift_col(value, d):
        return lax.ppermute(value, "col", [(j, (j + d) % n_col) for j in range(n_col)])

    row_index = lax.axis_index("row").astype(jnp.int32)
    col_index = lax.axis_index("col").astype(jnp.int32)
    my_c, my_b, my_a = row_index % n_c, row_index // n_c % n_b, row_index // (n_c * n_b)

    def piece(da, db, dc):
        return (dc * n_b + db) * n_a + da

    owner = block_cols // per_piece
    owner_c, owner_b, owner_a = owner % n_c, owner // n_c % n_b, owner // (n_c * n_b)
    place_cols = (
        piece((my_a - owner_a + n_a) % n_a, (my_b - owner_b + n_b) % n_b, (my_c - owner_c + n_c) % n_c) * per_piece
        + block_cols % per_piece
    )
    place_rows = (col_index - block_rows // per_piece + n_col) % n_col * per_piece + block_rows % per_piece
    live = jnp.arange(block_rows.shape[0], dtype=jnp.int32) < block_counts[0]
    put_cols = jnp.where(live, place_cols, n_row * per_piece)
    put_rows = jnp.where(live, place_rows, n_col * per_piece)

    mirror_outputs = [
        [piece(a, b, c) for a in range(n_a)] for c in range(n_c) for b in range(n_b)
    ]
    forward_outputs = [[j] for j in range(n_col)]

    def apply_operator(narrow):
        by_col = [narrow] + [shift_col(narrow, j) for j in range(1, n_col)]
        along_a = [narrow] + [shift(narrow, da=a) for a in range(1, n_a)]
        mirrors = block_product(
            0, mirror_outputs, [jnp.bfloat16] * len(mirror_outputs), n_row,
            block_counts, place_rows, put_cols, by_col, block_values,
        )
        along_a, mirrors = lax.optimization_barrier((along_a, mirrors))
        along_b = list(along_a)
        for b in range(1, n_b):
            along_b += [shift(part, db=b) for part in along_a]
        by_row = list(along_b)
        for c in range(1, n_c):
            by_row += [shift(part, dc=c) for part in along_b]

        by_b = []
        for b in range(n_b):
            share = mirrors[b].astype(jnp.float32)
            for c in range(1, n_c):
                share += shift(mirrors[c * n_b + b], dc=-c).astype(jnp.float32)
            by_b.append(share)
        share = by_b[0]
        for b in range(1, n_b):
            share += shift(by_b[b].astype(jnp.bfloat16), db=-b).astype(jnp.float32)
        mirror_sum = share[0]
        for a in range(1, n_a):
            mirror_sum += shift(share[a].astype(jnp.bfloat16), da=-a).astype(jnp.float32)

        forwards = block_product(
            1, forward_outputs, [jnp.float32] + [jnp.bfloat16] * (n_col - 1), n_col,
            block_counts, place_cols, put_rows, by_row, block_values,
        )
        forward_sum = forwards[0][0]
        for j in range(1, n_col):
            forward_sum += shift_col(forwards[j][0], -j).astype(jnp.float32)
        return forward_sum + mirror_sum

    current = (apply_operator(vectors.astype(jnp.bfloat16)) - center_value * vectors) / radius_value
    return 2.0 * (apply_operator(current.astype(jnp.bfloat16)) - center_value * current) / radius_value - vectors


def solution(mesh):
    return jax.shard_map(
        functools.partial(shards, mesh.shape["row"], mesh.shape["col"]),
        mesh=mesh,
        in_specs=(
            P(None, ("row", "col")),
            P(("row", "col"), None, None),
            P(("row", "col")),
            P(("row", "col")),
            P(("row", "col")),
            P(),
            P(),
        ),
        out_specs=P(None, ("row", "col")),
        check_vma=False,
    )
```

```python
import functools

import jax
import jax.numpy as jnp
from jax import lax
from jax.experimental import pallas as pl
from jax.experimental.pallas import tpu as pltpu
from jax.sharding import PartitionSpec as P

CHUNK = 32
UNROLL = 8


def product_kernel(contract, inputs, outputs, count_ref, take_ref, put_ref, *refs):
    n_in = len(inputs)
    pieces = refs[:n_in]
    blocks = refs[n_in]
    outs = refs[n_in + 1 : n_in + 1 + len(outputs)]
    held, held_blocks, total, block_sems = refs[n_in + 1 + len(outputs) :]
    capacity, size_block = blocks.shape[0], blocks.shape[1]
    per_piece = held.shape[2] // size_block
    chunks = capacity // CHUNK
    count = count_ref[0]

    def block_copy(g):
        part = pl.ds(g * CHUNK, CHUNK)
        return pltpu.make_async_copy(blocks.at[part], held_blocks.at[part], block_sems.at[g])

    for g in range(chunks):
        @pl.when(g * CHUNK < count)
        def _(g=g):
            block_copy(g).start()

    total[...] = jnp.zeros_like(total)
    for part, held_pieces in zip(pieces, inputs):
        for n, p in enumerate(held_pieces):
            held[p] = part[n]

    def group(first):
        places = []
        sums = []
        for n in range(UNROLL):
            slot = first + n
            take = take_ref[slot]
            put = put_ref[slot]
            column = pl.multiple_of((take % per_piece) * size_block, size_block)
            picked = held[take // per_piece, :, pl.ds(column, size_block)]
            sums.append(
                lax.dot_general(
                    picked, held_blocks[slot], (((1,), (contract,)), ((), ())), preferred_element_type=jnp.float32
                )
            )
            column = pl.multiple_of((put % per_piece) * size_block, size_block)
            places.append((put // per_piece, slice(None), pl.ds(column, size_block)))
        for place, value in zip(places, sums):
            total[place] += value

    for g in range(chunks):
        @pl.when(g * CHUNK < count)
        def _(g=g):
            block_copy(g).wait()

            @pl.loop(0, CHUNK // UNROLL)
            def _(n):
                group(g * CHUNK + n * UNROLL)

    for out, held_pieces in zip(outs, outputs):
        for n, p in enumerate(held_pieces):
            out[n] = total[p].astype(out.dtype)


def block_product(contract, inputs, outputs, dtypes, n_put, count, take, put, pieces, blocks):
    capacity, size_block = blocks.shape[0], blocks.shape[1]
    vector_count, own_rows = pieces[0].shape[-2:]
    pieces = [part.reshape(-1, vector_count, own_rows) for part in pieces]
    n_in = sum(part.shape[0] for part in pieces)
    smem = pl.BlockSpec(memory_space=pltpu.SMEM)
    vmem = pl.BlockSpec(memory_space=pltpu.VMEM)
    hbm = pl.BlockSpec(memory_space=pltpu.HBM)
    return pl.pallas_call(
        functools.partial(product_kernel, contract, inputs, outputs),
        out_shape=[
            jax.ShapeDtypeStruct((len(held), vector_count, own_rows), dtype) for held, dtype in zip(outputs, dtypes)
        ],
        in_specs=[smem] * 3 + [vmem] * len(pieces) + [hbm],
        out_specs=[pl.BlockSpec(memory_space=pltpu.VMEM)] * len(outputs),
        scratch_shapes=[
            pltpu.VMEM((n_in, vector_count, own_rows), jnp.bfloat16),
            pltpu.VMEM(blocks.shape, blocks.dtype),
            pltpu.VMEM((n_put + 1, vector_count, own_rows), jnp.float32),
            pltpu.SemaphoreType.DMA((capacity // CHUNK,)),
        ],
        compiler_params=pltpu.CompilerParams(vmem_limit_bytes=40 * 1024 * 1024),
        cost_estimate=pl.CostEstimate(
            flops=2 * capacity * size_block * size_block * 256,
            bytes_accessed=2 * blocks.size + 2 * n_in * vector_count * own_rows,
            transcendentals=0,
        ),
        name="mirror" if contract == 0 else "forward",
    )(count, take, put, *pieces, pltpu.with_memory_space_constraint(blocks, pltpu.HBM))


def shards(n_row, n_col, vectors, block_values, block_rows, block_cols, block_counts, center, radius):
    size_block = block_values.shape[1]
    own_rows = vectors.shape[1]
    per_piece = own_rows // size_block
    center_value = center[0]
    radius_value = radius[0]

    n_c = 2 if n_row % 2 == 0 else 1
    n_a = 4 if (n_row // n_c) % 4 == 0 else n_row // n_c
    n_b = n_row // n_c // n_a

    def at(a, b, c):
        return ((a % n_a) * n_b + b % n_b) * n_c + c % n_c

    spots = [(a, b, c) for a in range(n_a) for b in range(n_b) for c in range(n_c)]

    def shift(value, da=0, db=0, dc=0):
        pairs = [(at(a, b, c), at(a + da, b + db, c + dc)) for a, b, c in spots]
        return lax.ppermute(value, "row", pairs)

    def shift_col(value, d):
        return lax.ppermute(value, "col", [(j, (j + d) % n_col) for j in range(n_col)])

    row_index = lax.axis_index("row").astype(jnp.int32)
    col_index = lax.axis_index("col").astype(jnp.int32)
    my_c, my_b, my_a = row_index % n_c, row_index // n_c % n_b, row_index // (n_c * n_b)

    def piece(da, db, dc):
        return (dc * n_b + db) * n_a + da

    owner = block_cols // per_piece
    owner_c, owner_b, owner_a = owner % n_c, owner // n_c % n_b, owner // (n_c * n_b)
    place_cols = (
        piece((my_a - owner_a + n_a) % n_a, (my_b - owner_b + n_b) % n_b, (my_c - owner_c + n_c) % n_c) * per_piece
        + block_cols % per_piece
    )
    place_rows = (col_index - block_rows // per_piece + n_col) % n_col * per_piece + block_rows % per_piece
    live = jnp.arange(block_rows.shape[0], dtype=jnp.int32) < block_counts[0]
    put_cols = jnp.where(live, place_cols, n_row * per_piece)
    put_rows = jnp.where(live, place_rows, n_col * per_piece)

    mirror_outputs = [[piece(a, b, c) for b in range(n_b) for a in range(n_a)] for c in range(n_c)]
    forward_outputs = [[j] for j in range(n_col)]
    mirror_inputs = [[j] for j in range(n_col)]
    forward_inputs = []
    for c in range(n_c):
        forward_inputs.append([piece(0, b, c) for b in range(n_b)] + [piece(a, 0, c) for a in range(1, n_a)])
        if n_b > 1:
            forward_inputs.append([piece(a, b, c) for b in range(1, n_b) for a in range(1, n_a)])

    def apply_operator(narrow):
        by_col = [narrow] + [shift_col(narrow, j) for j in range(1, n_col)]
        near = [narrow] + [shift(narrow, db=b) for b in range(1, n_b)]
        far = [[shift(part, da=a) for a in range(1, n_a)] for part in near]
        mirrors = block_product(
            0, mirror_inputs, mirror_outputs, [jnp.bfloat16] * len(mirror_outputs), n_row,
            block_counts, place_rows, put_cols, by_col, block_values,
        )
        far[0], mirrors = lax.optimization_barrier((far[0], mirrors))

        shares = mirrors[0].astype(jnp.float32)
        for c in range(1, n_c):
            shares += shift(mirrors[c], dc=-c).astype(jnp.float32)
        by_b = [shares[b * n_a : (b + 1) * n_a] for b in range(n_b)]
        others = [shift(by_b[b].astype(jnp.bfloat16), db=-b) for b in range(1, n_b)]

        early = jnp.stack(near + far[0])
        late = [part for behind in far[1:] for part in behind]
        late = [jnp.stack(late)] if late else []
        by_row = [early] + late
        for c in range(1, n_c):
            by_row += [shift(part, dc=c) for part in [early] + late]
        by_row, others = lax.optimization_barrier((by_row, others))

        share = by_b[0]
        for other in others:
            share += other.astype(jnp.float32)
        back = [shift(share[a].astype(jnp.bfloat16), da=-a) for a in range(1, n_a)]

        forwards = block_product(
            1, forward_inputs, forward_outputs, [jnp.float32] + [jnp.bfloat16] * (n_col - 1), n_col,
            block_counts, place_cols, put_rows, by_row, block_values,
        )
        back, forwards = lax.optimization_barrier((back, forwards))
        forward_sum = forwards[0][0]
        for j in range(1, n_col):
            forward_sum += shift_col(forwards[j][0], -j).astype(jnp.float32)
        mirror_sum = share[0]
        for other in back:
            mirror_sum += other.astype(jnp.float32)
        return forward_sum + mirror_sum

    current = (apply_operator(vectors.astype(jnp.bfloat16)) - center_value * vectors) / radius_value
    return 2.0 * (apply_operator(current.astype(jnp.bfloat16)) - center_value * current) / radius_value - vectors


def solution(mesh):
    return jax.shard_map(
        functools.partial(shards, mesh.shape["row"], mesh.shape["col"]),
        mesh=mesh,
        in_specs=(
            P(None, ("row", "col")),
            P(("row", "col"), None, None),
            P(("row", "col")),
            P(("row", "col")),
            P(("row", "col")),
            P(),
            P(),
        ),
        out_specs=P(None, ("row", "col")),
        check_vma=False,
    )
```

```python
import functools

import jax
import jax.numpy as jnp
from jax import lax
from jax.experimental import pallas as pl
from jax.experimental.pallas import tpu as pltpu
from jax.sharding import PartitionSpec as P

CHUNK = 32
UNROLL = 8


def product_kernel(contract, inputs, outputs, count_ref, take_ref, put_ref, *refs):
    n_in = len(inputs)
    pieces = refs[:n_in]
    blocks = refs[n_in]
    outs = refs[n_in + 1 : n_in + 1 + len(outputs)]
    held, held_blocks, total, block_sems = refs[n_in + 1 + len(outputs) :]
    capacity, size_block = blocks.shape[0], blocks.shape[1]
    per_piece = held.shape[2] // size_block
    chunks = capacity // CHUNK
    count = count_ref[0]

    def block_copy(g):
        part = pl.ds(g * CHUNK, CHUNK)
        return pltpu.make_async_copy(blocks.at[part], held_blocks.at[part], block_sems.at[g])

    for g in range(chunks):
        @pl.when(g * CHUNK < count)
        def _(g=g):
            block_copy(g).start()

    total[...] = jnp.zeros_like(total)
    for part, held_pieces in zip(pieces, inputs):
        for n, p in enumerate(held_pieces):
            held[p] = part[n]

    def place(index):
        column = pl.multiple_of((index % per_piece) * size_block, size_block)
        return index // per_piece, slice(None), pl.ds(column, size_block)

    def group(first):
        products = []
        for n in range(0, UNROLL, 2):
            slot = first + n
            picked = jnp.concatenate([held[place(take_ref[slot])], held[place(take_ref[slot + 1])]], axis=0)
            if contract == 0:
                pair = jnp.concatenate([held_blocks[slot], held_blocks[slot + 1]], axis=1)
            else:
                pair = held_blocks[pl.ds(slot, 2)].reshape(2 * size_block, size_block)
            product = lax.dot_general(
                picked, pair, (((1,), (contract,)), ((), ())), preferred_element_type=jnp.float32
            )
            rows = product.shape[0] // 2
            products += [product[:rows, :size_block], product[rows:, size_block:]]
        for n, product in enumerate(products):
            total[place(put_ref[first + n])] += product

    for g in range(chunks):
        @pl.when(g * CHUNK < count)
        def _(g=g):
            block_copy(g).wait()

            @pl.loop(0, CHUNK // UNROLL)
            def _(n):
                group(g * CHUNK + n * UNROLL)

    for out, held_pieces in zip(outs, outputs):
        for n, p in enumerate(held_pieces):
            out[n] = total[p].astype(out.dtype)


def block_product(contract, inputs, outputs, dtypes, n_put, count, take, put, pieces, blocks):
    capacity, size_block = blocks.shape[0], blocks.shape[1]
    vector_count, own_rows = pieces[0].shape[-2:]
    pieces = [part.reshape(-1, vector_count, own_rows) for part in pieces]
    n_in = sum(part.shape[0] for part in pieces)
    smem = pl.BlockSpec(memory_space=pltpu.SMEM)
    vmem = pl.BlockSpec(memory_space=pltpu.VMEM)
    hbm = pl.BlockSpec(memory_space=pltpu.HBM)
    return pl.pallas_call(
        functools.partial(product_kernel, contract, inputs, outputs),
        out_shape=[
            jax.ShapeDtypeStruct((len(held), vector_count, own_rows), dtype) for held, dtype in zip(outputs, dtypes)
        ],
        in_specs=[smem] * 3 + [vmem] * len(pieces) + [hbm],
        out_specs=[pl.BlockSpec(memory_space=pltpu.VMEM)] * len(outputs),
        scratch_shapes=[
            pltpu.VMEM((n_in, vector_count, own_rows), jnp.bfloat16),
            pltpu.VMEM(blocks.shape, blocks.dtype),
            pltpu.VMEM((n_put + 1, vector_count, own_rows), jnp.float32),
            pltpu.SemaphoreType.DMA((capacity // CHUNK,)),
        ],
        compiler_params=pltpu.CompilerParams(vmem_limit_bytes=40 * 1024 * 1024),
        cost_estimate=pl.CostEstimate(
            flops=2 * capacity * size_block * size_block * 256,
            bytes_accessed=2 * blocks.size + 2 * n_in * vector_count * own_rows,
            transcendentals=0,
        ),
        name="mirror" if contract == 0 else "forward",
    )(count, take, put, *pieces, pltpu.with_memory_space_constraint(blocks, pltpu.HBM))


def shards(n_row, n_col, vectors, block_values, block_rows, block_cols, block_counts, center, radius):
    size_block = block_values.shape[1]
    own_rows = vectors.shape[1]
    per_piece = own_rows // size_block
    center_value = center[0]
    radius_value = radius[0]

    n_c = 2 if n_row % 2 == 0 else 1
    n_a = 4 if (n_row // n_c) % 4 == 0 else n_row // n_c
    n_b = n_row // n_c // n_a

    def at(a, b, c):
        return ((a % n_a) * n_b + b % n_b) * n_c + c % n_c

    spots = [(a, b, c) for a in range(n_a) for b in range(n_b) for c in range(n_c)]

    def shift(value, da=0, db=0, dc=0):
        pairs = [(at(a, b, c), at(a + da, b + db, c + dc)) for a, b, c in spots]
        return lax.ppermute(value, "row", pairs)

    def shift_col(value, d):
        return lax.ppermute(value, "col", [(j, (j + d) % n_col) for j in range(n_col)])

    row_index = lax.axis_index("row").astype(jnp.int32)
    col_index = lax.axis_index("col").astype(jnp.int32)
    my_c, my_b, my_a = row_index % n_c, row_index // n_c % n_b, row_index // (n_c * n_b)

    def piece(da, db, dc):
        return (dc * n_b + db) * n_a + da

    owner = block_cols // per_piece
    owner_c, owner_b, owner_a = owner % n_c, owner // n_c % n_b, owner // (n_c * n_b)
    place_cols = (
        piece((my_a - owner_a + n_a) % n_a, (my_b - owner_b + n_b) % n_b, (my_c - owner_c + n_c) % n_c) * per_piece
        + block_cols % per_piece
    )
    place_rows = (col_index - block_rows // per_piece + n_col) % n_col * per_piece + block_rows % per_piece
    live = jnp.arange(block_rows.shape[0], dtype=jnp.int32) < block_counts[0]
    put_cols = jnp.where(live, place_cols, n_row * per_piece)
    put_rows = jnp.where(live, place_rows, n_col * per_piece)

    mirror_outputs = [[piece(a, b, c) for b in range(n_b) for a in range(n_a)] for c in range(n_c)]
    forward_outputs = [[j] for j in range(n_col)]
    mirror_inputs = [[j] for j in range(n_col)]
    forward_inputs = []
    for c in range(n_c):
        forward_inputs.append([piece(0, b, c) for b in range(n_b)] + [piece(a, 0, c) for a in range(1, n_a)])
        if n_b > 1:
            forward_inputs.append([piece(a, b, c) for b in range(1, n_b) for a in range(1, n_a)])

    def apply_operator(narrow):
        by_col = [narrow] + [shift_col(narrow, j) for j in range(1, n_col)]
        near = [narrow] + [shift(narrow, db=b) for b in range(1, n_b)]
        far = [[shift(part, da=a) for a in range(1, n_a)] for part in near]
        mirrors = block_product(
            0, mirror_inputs, mirror_outputs, [jnp.bfloat16] * len(mirror_outputs), n_row,
            block_counts, place_rows, put_cols, by_col, block_values,
        )
        far[0], mirrors = lax.optimization_barrier((far[0], mirrors))

        shares = mirrors[0].astype(jnp.float32)
        for c in range(1, n_c):
            shares += shift(mirrors[c], dc=-c).astype(jnp.float32)
        by_b = [shares[b * n_a : (b + 1) * n_a] for b in range(n_b)]
        others = [shift(by_b[b].astype(jnp.bfloat16), db=-b) for b in range(1, n_b)]

        early = jnp.stack(near + far[0])
        late = [part for behind in far[1:] for part in behind]
        late = [jnp.stack(late)] if late else []
        by_row = [early] + late
        for c in range(1, n_c):
            by_row += [shift(part, dc=c) for part in [early] + late]
        by_row, others = lax.optimization_barrier((by_row, others))

        share = by_b[0]
        for other in others:
            share += other.astype(jnp.float32)
        back = [shift(share[a].astype(jnp.bfloat16), da=-a) for a in range(1, n_a)]

        forwards = block_product(
            1, forward_inputs, forward_outputs, [jnp.float32] + [jnp.bfloat16] * (n_col - 1), n_col,
            block_counts, place_cols, put_rows, by_row, block_values,
        )
        back, forwards = lax.optimization_barrier((back, forwards))
        forward_sum = forwards[0][0]
        for j in range(1, n_col):
            forward_sum += shift_col(forwards[j][0], -j).astype(jnp.float32)
        mirror_sum = share[0]
        for other in back:
            mirror_sum += other.astype(jnp.float32)
        return forward_sum + mirror_sum

    current = (apply_operator(vectors.astype(jnp.bfloat16)) - center_value * vectors) / radius_value
    return 2.0 * (apply_operator(current.astype(jnp.bfloat16)) - center_value * current) / radius_value - vectors


def solution(mesh):
    return jax.shard_map(
        functools.partial(shards, mesh.shape["row"], mesh.shape["col"]),
        mesh=mesh,
        in_specs=(
            P(None, ("row", "col")),
            P(("row", "col"), None, None),
            P(("row", "col")),
            P(("row", "col")),
            P(("row", "col")),
            P(),
            P(),
        ),
        out_specs=P(None, ("row", "col")),
        check_vma=False,
    )
```

```python
import functools

import jax
import jax.numpy as jnp
from jax import lax
from jax.experimental import pallas as pl
from jax.experimental.pallas import tpu as pltpu
from jax.sharding import PartitionSpec as P

CHUNK = 32
UNROLL = 32


def product_kernel(contract, inputs, outputs, count_ref, take_ref, put_ref, *refs):
    n_in = len(inputs)
    pieces = refs[:n_in]
    blocks = refs[n_in]
    outs = refs[n_in + 1 : n_in + 1 + len(outputs)]
    held, held_blocks, total, block_sems = refs[n_in + 1 + len(outputs) :]
    capacity, size_block = blocks.shape[0], blocks.shape[1]
    per_piece = held.shape[2] // size_block
    chunks = capacity // CHUNK
    count = count_ref[0]

    def block_copy(g):
        part = pl.ds(g * CHUNK, CHUNK)
        return pltpu.make_async_copy(blocks.at[part], held_blocks.at[part], block_sems.at[g])

    for g in range(chunks):
        @pl.when(g * CHUNK < count)
        def _(g=g):
            block_copy(g).start()

    total[...] = jnp.zeros_like(total)
    for part, held_pieces in zip(pieces, inputs):
        for n, p in enumerate(held_pieces):
            held[p] = part[n]

    def place(index):
        column = pl.multiple_of((index % per_piece) * size_block, size_block)
        return index // per_piece, slice(None), pl.ds(column, size_block)

    def group(first):
        products = []
        for n in range(0, UNROLL, 2):
            slot = first + n
            picked = jnp.concatenate([held[place(take_ref[slot])], held[place(take_ref[slot + 1])]], axis=0)
            if contract == 0:
                pair = jnp.concatenate([held_blocks[slot], held_blocks[slot + 1]], axis=1)
            else:
                pair = held_blocks[pl.ds(slot, 2)].reshape(2 * size_block, size_block)
            product = lax.dot_general(
                picked, pair, (((1,), (contract,)), ((), ())), preferred_element_type=jnp.float32
            )
            rows = product.shape[0] // 2
            products += [product[:rows, :size_block], product[rows:, size_block:]]
        for n, product in enumerate(products):
            total[place(put_ref[first + n])] += product

    @pl.loop(0, (count + CHUNK - 1) // CHUNK)
    def _(g):
        block_copy(g).wait()
        for n in range(0, CHUNK, UNROLL):
            group(g * CHUNK + n)

    for out, held_pieces in zip(outs, outputs):
        for n, p in enumerate(held_pieces):
            out[n] = total[p].astype(out.dtype)


def block_product(contract, inputs, outputs, dtypes, n_put, count, take, put, pieces, blocks):
    capacity, size_block = blocks.shape[0], blocks.shape[1]
    vector_count, own_rows = pieces[0].shape[-2:]
    pieces = [part.reshape(-1, vector_count, own_rows) for part in pieces]
    n_in = sum(part.shape[0] for part in pieces)
    smem = pl.BlockSpec(memory_space=pltpu.SMEM)
    vmem = pl.BlockSpec(memory_space=pltpu.VMEM)
    hbm = pl.BlockSpec(memory_space=pltpu.HBM)
    return pl.pallas_call(
        functools.partial(product_kernel, contract, inputs, outputs),
        out_shape=[
            jax.ShapeDtypeStruct((len(held), vector_count, own_rows), dtype) for held, dtype in zip(outputs, dtypes)
        ],
        in_specs=[smem] * 3 + [vmem] * len(pieces) + [hbm],
        out_specs=[pl.BlockSpec(memory_space=pltpu.VMEM)] * len(outputs),
        scratch_shapes=[
            pltpu.VMEM((n_in, vector_count, own_rows), jnp.bfloat16),
            pltpu.VMEM(blocks.shape, blocks.dtype),
            pltpu.VMEM((n_put + 1, vector_count, own_rows), jnp.float32),
            pltpu.SemaphoreType.DMA((capacity // CHUNK,)),
        ],
        compiler_params=pltpu.CompilerParams(vmem_limit_bytes=40 * 1024 * 1024),
        cost_estimate=pl.CostEstimate(
            flops=2 * capacity * size_block * size_block * 256,
            bytes_accessed=2 * blocks.size + 2 * n_in * vector_count * own_rows,
            transcendentals=0,
        ),
        name="mirror" if contract == 0 else "forward",
    )(count, take, put, *pieces, pltpu.with_memory_space_constraint(blocks, pltpu.HBM))


def shards(n_row, n_col, vectors, block_values, block_rows, block_cols, block_counts, center, radius):
    size_block = block_values.shape[1]
    own_rows = vectors.shape[1]
    per_piece = own_rows // size_block
    center_value = center[0]
    radius_value = radius[0]

    n_c = 2 if n_row % 2 == 0 else 1
    n_a = 4 if (n_row // n_c) % 4 == 0 else n_row // n_c
    n_b = n_row // n_c // n_a

    def at(a, b, c):
        return ((a % n_a) * n_b + b % n_b) * n_c + c % n_c

    spots = [(a, b, c) for a in range(n_a) for b in range(n_b) for c in range(n_c)]

    def shift(value, da=0, db=0, dc=0):
        pairs = [(at(a, b, c), at(a + da, b + db, c + dc)) for a, b, c in spots]
        return lax.ppermute(value, "row", pairs)

    def shift_col(value, d):
        return lax.ppermute(value, "col", [(j, (j + d) % n_col) for j in range(n_col)])

    row_index = lax.axis_index("row").astype(jnp.int32)
    col_index = lax.axis_index("col").astype(jnp.int32)
    my_c, my_b, my_a = row_index % n_c, row_index // n_c % n_b, row_index // (n_c * n_b)

    def piece(da, db, dc):
        return (dc * n_b + db) * n_a + da

    owner = block_cols // per_piece
    owner_c, owner_b, owner_a = owner % n_c, owner // n_c % n_b, owner // (n_c * n_b)
    place_cols = (
        piece((my_a - owner_a + n_a) % n_a, (my_b - owner_b + n_b) % n_b, (my_c - owner_c + n_c) % n_c) * per_piece
        + block_cols % per_piece
    )
    place_rows = (col_index - block_rows // per_piece + n_col) % n_col * per_piece + block_rows % per_piece
    live = jnp.arange(block_rows.shape[0], dtype=jnp.int32) < block_counts[0]
    put_cols = jnp.where(live, place_cols, n_row * per_piece)
    put_rows = jnp.where(live, place_rows, n_col * per_piece)

    mirror_outputs = [[piece(a, b, c) for b in range(n_b) for a in range(n_a)] for c in range(n_c)]
    forward_outputs = [[j] for j in range(n_col)]
    mirror_inputs = [[j] for j in range(n_col)]
    forward_inputs = []
    for c in range(n_c):
        forward_inputs.append([piece(0, b, c) for b in range(n_b)] + [piece(a, 0, c) for a in range(1, n_a)])
        if n_b > 1:
            forward_inputs.append([piece(a, b, c) for b in range(1, n_b) for a in range(1, n_a)])

    def apply_operator(narrow):
        by_col = [narrow] + [shift_col(narrow, j) for j in range(1, n_col)]
        near = [narrow] + [shift(narrow, db=b) for b in range(1, n_b)]
        far = [[shift(part, da=a) for a in range(1, n_a)] for part in near]
        mirrors = block_product(
            0, mirror_inputs, mirror_outputs, [jnp.bfloat16] * len(mirror_outputs), n_row,
            block_counts, place_rows, put_cols, by_col, block_values,
        )
        far[0], mirrors = lax.optimization_barrier((far[0], mirrors))

        shares = mirrors[0].astype(jnp.float32)
        for c in range(1, n_c):
            shares += shift(mirrors[c], dc=-c).astype(jnp.float32)
        by_b = [shares[b * n_a : (b + 1) * n_a] for b in range(n_b)]
        others = [shift(by_b[b].astype(jnp.bfloat16), db=-b) for b in range(1, n_b)]

        early = jnp.stack(near + far[0])
        late = [part for behind in far[1:] for part in behind]
        late = [jnp.stack(late)] if late else []
        by_row = [early] + late
        for c in range(1, n_c):
            by_row += [shift(part, dc=c) for part in [early] + late]
        by_row, others = lax.optimization_barrier((by_row, others))

        share = by_b[0]
        for other in others:
            share += other.astype(jnp.float32)
        back = [shift(share[a].astype(jnp.bfloat16), da=-a) for a in range(1, n_a)]

        forwards = block_product(
            1, forward_inputs, forward_outputs, [jnp.float32] + [jnp.bfloat16] * (n_col - 1), n_col,
            block_counts, place_cols, put_rows, by_row, block_values,
        )
        back, forwards = lax.optimization_barrier((back, forwards))
        forward_sum = forwards[0][0]
        for j in range(1, n_col):
            forward_sum += shift_col(forwards[j][0], -j).astype(jnp.float32)
        mirror_sum = share[0]
        for other in back:
            mirror_sum += other.astype(jnp.float32)
        return forward_sum + mirror_sum

    current = (apply_operator(vectors.astype(jnp.bfloat16)) - center_value * vectors) / radius_value
    return 2.0 * (apply_operator(current.astype(jnp.bfloat16)) - center_value * current) / radius_value - vectors


def solution(mesh):
    return jax.shard_map(
        functools.partial(shards, mesh.shape["row"], mesh.shape["col"]),
        mesh=mesh,
        in_specs=(
            P(None, ("row", "col")),
            P(("row", "col"), None, None),
            P(("row", "col")),
            P(("row", "col")),
            P(("row", "col")),
            P(),
            P(),
        ),
        out_specs=P(None, ("row", "col")),
        check_vma=False,
    )
```

```python
import functools

import jax
import jax.numpy as jnp
from jax import lax
from jax.experimental import pallas as pl
from jax.experimental.pallas import tpu as pltpu
from jax.sharding import PartitionSpec as P

CHUNK = 32
UNROLL = 32


def product_kernel(contract, inputs, outputs, count_ref, take_ref, put_ref, *refs):
    n_in = len(inputs)
    pieces = refs[:n_in]
    blocks = refs[n_in]
    outs = refs[n_in + 1 : n_in + 1 + len(outputs)]
    held, held_blocks, total, block_sems = refs[n_in + 1 + len(outputs) :]
    capacity, size_block = blocks.shape[0], blocks.shape[1]
    per_piece = held.shape[2] // size_block
    chunks = capacity // CHUNK
    count = count_ref[0]

    def block_copy(g):
        part = pl.ds(g * CHUNK, CHUNK)
        return pltpu.make_async_copy(blocks.at[part], held_blocks.at[part], block_sems.at[g])

    for g in range(chunks):
        @pl.when(g * CHUNK < count)
        def _(g=g):
            block_copy(g).start()

    total[...] = jnp.zeros_like(total)
    for part, held_pieces in zip(pieces, inputs):
        for n, p in enumerate(held_pieces):
            held[p] = part[n]

    def place(index):
        column = pl.multiple_of((index % per_piece) * size_block, size_block)
        return index // per_piece, slice(None), pl.ds(column, size_block)

    def group(first):
        products = []
        for n in range(0, UNROLL, 2):
            slot = first + n
            picked = jnp.concatenate([held[place(take_ref[slot])], held[place(take_ref[slot + 1])]], axis=0)
            if contract == 0:
                pair = jnp.concatenate([held_blocks[slot], held_blocks[slot + 1]], axis=1)
            else:
                pair = held_blocks[pl.ds(slot, 2)].reshape(2 * size_block, size_block)
            product = lax.dot_general(
                picked, pair, (((1,), (contract,)), ((), ())), preferred_element_type=jnp.float32
            )
            rows = product.shape[0] // 2
            products += [product[:rows, :size_block], product[rows:, size_block:]]
        for n, product in enumerate(products):
            total[place(put_ref[first + n])] += product

    @pl.loop(0, (count + CHUNK - 1) // CHUNK)
    def _(g):
        block_copy(g).wait()
        for n in range(0, CHUNK, UNROLL):
            group(g * CHUNK + n)

    for out, held_pieces in zip(outs, outputs):
        for n, p in enumerate(held_pieces):
            out[n] = total[p].astype(out.dtype)


def block_product(contract, inputs, outputs, dtypes, n_put, count, take, put, pieces, blocks):
    capacity, size_block = blocks.shape[0], blocks.shape[1]
    vector_count, own_rows = pieces[0].shape[-2:]
    pieces = [part.reshape(-1, vector_count, own_rows) for part in pieces]
    n_in = sum(part.shape[0] for part in pieces)
    smem = pl.BlockSpec(memory_space=pltpu.SMEM)
    vmem = pl.BlockSpec(memory_space=pltpu.VMEM)
    hbm = pl.BlockSpec(memory_space=pltpu.HBM)
    return pl.pallas_call(
        functools.partial(product_kernel, contract, inputs, outputs),
        out_shape=[
            jax.ShapeDtypeStruct((len(held), vector_count, own_rows), dtype) for held, dtype in zip(outputs, dtypes)
        ],
        in_specs=[smem] * 3 + [vmem] * len(pieces) + [hbm],
        out_specs=[pl.BlockSpec(memory_space=pltpu.VMEM)] * len(outputs),
        scratch_shapes=[
            pltpu.VMEM((n_in, vector_count, own_rows), jnp.bfloat16),
            pltpu.VMEM(blocks.shape, blocks.dtype),
            pltpu.VMEM((n_put + 1, vector_count, own_rows), jnp.float32),
            pltpu.SemaphoreType.DMA((capacity // CHUNK,)),
        ],
        compiler_params=pltpu.CompilerParams(vmem_limit_bytes=40 * 1024 * 1024),
        cost_estimate=pl.CostEstimate(
            flops=2 * capacity * size_block * size_block * 256,
            bytes_accessed=2 * blocks.size + 2 * n_in * vector_count * own_rows,
            transcendentals=0,
        ),
        name="mirror" if contract == 0 else "forward",
    )(count, take, put, *pieces, pltpu.with_memory_space_constraint(blocks, pltpu.HBM))


def shards(n_row, n_col, vectors, block_values, block_rows, block_cols, block_counts, center, radius):
    size_block = block_values.shape[1]
    own_rows = vectors.shape[1]
    per_piece = own_rows // size_block
    center_value = center[0]
    radius_value = radius[0]

    n_c = 2 if n_row % 2 == 0 else 1
    n_a = 4 if (n_row // n_c) % 4 == 0 else n_row // n_c
    n_b = n_row // n_c // n_a

    def at(a, b, c):
        return ((a % n_a) * n_b + b % n_b) * n_c + c % n_c

    spots = [(a, b, c) for a in range(n_a) for b in range(n_b) for c in range(n_c)]

    def shift(value, da=0, db=0, dc=0):
        pairs = [(at(a, b, c), at(a + da, b + db, c + dc)) for a, b, c in spots]
        return lax.ppermute(value, "row", pairs)

    def shift_col(value, d):
        return lax.ppermute(value, "col", [(j, (j + d) % n_col) for j in range(n_col)])

    row_index = lax.axis_index("row").astype(jnp.int32)
    col_index = lax.axis_index("col").astype(jnp.int32)
    my_c, my_b, my_a = row_index % n_c, row_index // n_c % n_b, row_index // (n_c * n_b)

    def piece(da, db, dc):
        return (dc * n_b + db) * n_a + da

    owner = block_cols // per_piece
    owner_c, owner_b, owner_a = owner % n_c, owner // n_c % n_b, owner // (n_c * n_b)
    place_cols = (
        piece((my_a - owner_a + n_a) % n_a, (my_b - owner_b + n_b) % n_b, (my_c - owner_c + n_c) % n_c) * per_piece
        + block_cols % per_piece
    )
    place_rows = (col_index - block_rows // per_piece + n_col) % n_col * per_piece + block_rows % per_piece
    live = jnp.arange(block_rows.shape[0], dtype=jnp.int32) < block_counts[0]
    put_cols = jnp.where(live, place_cols, n_row * per_piece)
    put_rows = jnp.where(live, place_rows, n_col * per_piece)

    mirror_outputs = [[piece(a, b, c) for b in range(n_b) for a in range(n_a)] for c in range(n_c)]
    forward_outputs = [[j] for j in range(n_col)]
    mirror_inputs = [[j] for j in range(n_col)]
    forward_inputs = []
    for c in range(n_c):
        forward_inputs.append([piece(0, b, c) for b in range(n_b)] + [piece(a, 0, c) for a in range(1, n_a)])
        if n_b > 1:
            forward_inputs.append([piece(a, b, c) for b in range(1, n_b) for a in range(1, n_a)])

    def apply_operator(narrow):
        by_col = [narrow] + [shift_col(narrow, j) for j in range(1, n_col)]
        near = [narrow] + [shift(narrow, db=b) for b in range(1, n_b)]
        far = [[shift(part, da=a) for a in range(1, n_a)] for part in near]
        mirrors = block_product(
            0, mirror_inputs, mirror_outputs, [jnp.bfloat16] * len(mirror_outputs), n_row,
            block_counts, place_rows, put_cols, by_col, block_values,
        )
        far[0], mirrors = lax.optimization_barrier((far[0], mirrors))

        shares = mirrors[0].astype(jnp.float32)
        for c in range(1, n_c):
            shares += shift(mirrors[c], dc=-c).astype(jnp.float32)
        by_b = [shares[b * n_a : (b + 1) * n_a] for b in range(n_b)]
        others = [shift(by_b[b].astype(jnp.bfloat16), db=-b) for b in range(1, n_b)]

        early = jnp.stack(near + far[0])
        late = [part for behind in far[1:] for part in behind]
        late = [jnp.stack(late)] if late else []
        by_row = [early] + late
        for c in range(1, n_c):
            by_row += [shift(part, dc=c) for part in [early] + late]
        by_row, others = lax.optimization_barrier((by_row, others))

        share = by_b[0]
        for other in others:
            share += other.astype(jnp.float32)
        back = [shift(share[a].astype(jnp.bfloat16), da=-a) for a in range(1, n_a)]

        forwards = block_product(
            1, forward_inputs, forward_outputs, [jnp.float32] + [jnp.bfloat16] * (n_col - 1), n_col,
            block_counts, place_cols, put_rows, by_row, block_values,
        )
        back, own = lax.optimization_barrier((back, forwards[0]))
        forward_sum = own[0]
        for j in range(1, n_col):
            forward_sum += shift_col(forwards[j][0], -j).astype(jnp.float32)
        mirror_sum = share[0]
        for other in back:
            mirror_sum += other.astype(jnp.float32)
        return forward_sum + mirror_sum

    current = (apply_operator(vectors.astype(jnp.bfloat16)) - center_value * vectors) / radius_value
    return 2.0 * (apply_operator(current.astype(jnp.bfloat16)) - center_value * current) / radius_value - vectors


def solution(mesh):
    return jax.shard_map(
        functools.partial(shards, mesh.shape["row"], mesh.shape["col"]),
        mesh=mesh,
        in_specs=(
            P(None, ("row", "col")),
            P(("row", "col"), None, None),
            P(("row", "col")),
            P(("row", "col")),
            P(("row", "col")),
            P(),
            P(),
        ),
        out_specs=P(None, ("row", "col")),
        check_vma=False,
    )
```

```python
import functools

import jax
import jax.numpy as jnp
from jax import lax
from jax.experimental import pallas as pl
from jax.experimental.pallas import tpu as pltpu
from jax.sharding import PartitionSpec as P

CHUNK = 32
UNROLL = 32


def product_kernel(contract, inputs, outputs, count_ref, take_ref, put_ref, *refs):
    n_in = len(inputs)
    pieces = refs[:n_in]
    blocks = refs[n_in]
    outs = refs[n_in + 1 : n_in + 1 + len(outputs)]
    held, held_blocks, total, block_sems = refs[n_in + 1 + len(outputs) :]
    capacity, size_block = blocks.shape[0], blocks.shape[1]
    per_piece = held.shape[2] // size_block
    chunks = capacity // CHUNK
    count = count_ref[0]

    def block_copy(g):
        part = pl.ds(g * CHUNK, CHUNK)
        return pltpu.make_async_copy(blocks.at[part], held_blocks.at[part], block_sems.at[g])

    for g in range(chunks):
        @pl.when(g * CHUNK < count)
        def _(g=g):
            block_copy(g).start()

    total[...] = jnp.zeros_like(total)
    for part, held_pieces in zip(pieces, inputs):
        for n, p in enumerate(held_pieces):
            held[p] = part[n]

    def place(index):
        column = pl.multiple_of((index % per_piece) * size_block, size_block)
        return index // per_piece, slice(None), pl.ds(column, size_block)

    def group(first):
        products = []
        for n in range(0, UNROLL, 2):
            slot = first + n
            picked = jnp.concatenate([held[place(take_ref[slot])], held[place(take_ref[slot + 1])]], axis=0)
            if contract == 0:
                pair = jnp.concatenate([held_blocks[slot], held_blocks[slot + 1]], axis=1)
            else:
                pair = held_blocks[pl.ds(slot, 2)].reshape(2 * size_block, size_block)
            product = lax.dot_general(
                picked, pair, (((1,), (contract,)), ((), ())), preferred_element_type=jnp.float32
            )
            rows = product.shape[0] // 2
            products += [product[:rows, :size_block], product[rows:, size_block:]]
        for n, product in enumerate(products):
            total[place(put_ref[first + n])] += product

    @pl.loop(0, (count + CHUNK - 1) // CHUNK)
    def _(g):
        block_copy(g).wait()
        for n in range(0, CHUNK, UNROLL):
            group(g * CHUNK + n)

    for out, held_pieces in zip(outs, outputs):
        for n, p in enumerate(held_pieces):
            out[n] = total[p].astype(out.dtype)


def block_product(contract, inputs, outputs, dtypes, n_put, count, take, put, pieces, blocks):
    capacity, size_block = blocks.shape[0], blocks.shape[1]
    vector_count, own_rows = pieces[0].shape[-2:]
    pieces = [part.reshape(-1, vector_count, own_rows) for part in pieces]
    n_in = sum(part.shape[0] for part in pieces)
    smem = pl.BlockSpec(memory_space=pltpu.SMEM)
    vmem = pl.BlockSpec(memory_space=pltpu.VMEM)
    hbm = pl.BlockSpec(memory_space=pltpu.HBM)
    return pl.pallas_call(
        functools.partial(product_kernel, contract, inputs, outputs),
        out_shape=[
            jax.ShapeDtypeStruct((len(held), vector_count, own_rows), dtype) for held, dtype in zip(outputs, dtypes)
        ],
        in_specs=[smem] * 3 + [vmem] * len(pieces) + [hbm],
        out_specs=[pl.BlockSpec(memory_space=pltpu.VMEM)] * len(outputs),
        scratch_shapes=[
            pltpu.VMEM((n_in, vector_count, own_rows), jnp.bfloat16),
            pltpu.VMEM(blocks.shape, blocks.dtype),
            pltpu.VMEM((n_put + 1, vector_count, own_rows), jnp.float32),
            pltpu.SemaphoreType.DMA((capacity // CHUNK,)),
        ],
        compiler_params=pltpu.CompilerParams(vmem_limit_bytes=40 * 1024 * 1024),
        cost_estimate=pl.CostEstimate(
            flops=2 * capacity * size_block * size_block * 256,
            bytes_accessed=2 * blocks.size + 2 * n_in * vector_count * own_rows,
            transcendentals=0,
        ),
        name="mirror" if contract == 0 else "forward",
    )(count, take, put, *pieces, pltpu.with_memory_space_constraint(blocks, pltpu.HBM))


def shards(n_row, n_col, vectors, block_values, block_rows, block_cols, block_counts, center, radius):
    size_block = block_values.shape[1]
    own_rows = vectors.shape[1]
    per_piece = own_rows // size_block
    center_value = center[0]
    radius_value = radius[0]

    n_c = 2 if n_row % 2 == 0 else 1
    n_a = 4 if (n_row // n_c) % 4 == 0 else n_row // n_c
    n_b = n_row // n_c // n_a

    def at(a, b, c):
        return ((a % n_a) * n_b + b % n_b) * n_c + c % n_c

    spots = [(a, b, c) for a in range(n_a) for b in range(n_b) for c in range(n_c)]

    def shift(value, da=0, db=0, dc=0):
        pairs = [(at(a, b, c), at(a + da, b + db, c + dc)) for a, b, c in spots]
        return lax.ppermute(value, "row", pairs)

    def shift_col(value, d):
        return lax.ppermute(value, "col", [(j, (j + d) % n_col) for j in range(n_col)])

    row_index = lax.axis_index("row").astype(jnp.int32)
    col_index = lax.axis_index("col").astype(jnp.int32)
    my_c, my_b, my_a = row_index % n_c, row_index // n_c % n_b, row_index // (n_c * n_b)

    def piece(da, db, dc):
        return (dc * n_b + db) * n_a + da

    owner = block_cols // per_piece
    owner_c, owner_b, owner_a = owner % n_c, owner // n_c % n_b, owner // (n_c * n_b)
    place_cols = (
        piece((my_a - owner_a + n_a) % n_a, (my_b - owner_b + n_b) % n_b, (my_c - owner_c + n_c) % n_c) * per_piece
        + block_cols % per_piece
    )
    place_rows = (col_index - block_rows // per_piece + n_col) % n_col * per_piece + block_rows % per_piece
    live = jnp.arange(block_rows.shape[0], dtype=jnp.int32) < block_counts[0]
    put_cols = jnp.where(live, place_cols, n_row * per_piece)
    put_rows = jnp.where(live, place_rows, n_col * per_piece)

    order = list(range(1, n_a)) + [0]
    halves = [order[: n_a // 2], order[n_a // 2 :]] if n_a > 1 else [order]
    mirror_outputs = [[piece(a, b, c) for b in range(n_b) for a in order] for c in range(n_c)]
    forward_outputs = [[j] for j in range(n_col)]
    mirror_inputs = [[j] for j in range(n_col)]
    forward_inputs = []
    for c in range(n_c):
        forward_inputs.append([piece(a, 0, c) for a in range(n_a)])
        if n_b > 1:
            forward_inputs.append([piece(a, b, c) for b in range(1, n_b) for a in range(n_a)])

    def apply_operator(narrow):
        by_col = [narrow] + [shift_col(narrow, j) for j in range(1, n_col)]
        along_a = [shift(narrow, da=a) for a in range(1, n_a)]
        along_b = [shift(narrow, db=b) for b in range(1, n_b)]
        mirrors = block_product(
            0, mirror_inputs, mirror_outputs, [jnp.bfloat16] * len(mirror_outputs), n_row,
            block_counts, place_rows, put_cols, by_col, block_values,
        )
        by_col, along_a, along_b, mirrors = lax.optimization_barrier((by_col, along_a, along_b, mirrors))

        shares = mirrors[0].astype(jnp.float32)
        for c in range(1, n_c):
            shares += shift(mirrors[c], dc=-c).astype(jnp.float32)
        parts = []
        for b in range(n_b):
            first = b * n_a
            for half in halves:
                parts.append(shares[first : first + len(half)])
                first += len(half)
        kept = parts[: len(halves)]
        sends = [part.astype(jnp.bfloat16) for part in parts[len(halves) :]]

        early = jnp.stack([narrow] + along_a)
        along_both = [shift(early[1:], db=b) for b in range(1, n_b)]
        sends, along_both = lax.optimization_barrier((sends, along_both))
        others = [shift(send, db=-(n // len(halves) + 1)) for n, send in enumerate(sends)]
        by_row = [early]
        if n_b > 1:
            late = []
            for one, rest in zip(along_b, along_both):
                late += [one[None], rest]
            by_row.append(jnp.concatenate(late))
        for c in range(1, n_c):
            by_row += [shift(part, dc=c) for part in by_row[: len(by_row) // c]]
        forwards = block_product(
            1, forward_inputs, forward_outputs, [jnp.float32] + [jnp.bfloat16] * (n_col - 1), n_col,
            block_counts, place_cols, put_rows, by_row, block_values,
        )
        others, own = lax.optimization_barrier((others, forwards[0]))

        mirror_sum = 0.0
        for h, half in enumerate(halves):
            share = kept[h]
            for other in others[h :: len(halves)]:
                share += other.astype(jnp.float32)
            for n, a in enumerate(half):
                mirror_sum += shift(share[n].astype(jnp.bfloat16), da=-a).astype(jnp.float32) if a else share[n]
        forward_sum = own[0]
        for j in range(1, n_col):
            forward_sum += shift_col(forwards[j][0], -j).astype(jnp.float32)
        return forward_sum + mirror_sum

    current = (apply_operator(vectors.astype(jnp.bfloat16)) - center_value * vectors) / radius_value
    return 2.0 * (apply_operator(current.astype(jnp.bfloat16)) - center_value * current) / radius_value - vectors


def solution(mesh):
    return jax.shard_map(
        functools.partial(shards, mesh.shape["row"], mesh.shape["col"]),
        mesh=mesh,
        in_specs=(
            P(None, ("row", "col")),
            P(("row", "col"), None, None),
            P(("row", "col")),
            P(("row", "col")),
            P(("row", "col")),
            P(),
            P(),
        ),
        out_specs=P(None, ("row", "col")),
        check_vma=False,
    )
```

```python
import functools

import jax
import jax.numpy as jnp
from jax import lax
from jax.experimental import pallas as pl
from jax.experimental.pallas import tpu as pltpu
from jax.sharding import PartitionSpec as P

CHUNK = 32
UNROLL = 32


def product_kernel(contract, inputs, outputs, count_ref, take_ref, put_ref, *refs):
    n_in = len(inputs)
    pieces = refs[:n_in]
    blocks = refs[n_in]
    outs = refs[n_in + 1 : n_in + 1 + len(outputs)]
    held, held_blocks, total, block_sems = refs[n_in + 1 + len(outputs) :]
    capacity, size_block = blocks.shape[0], blocks.shape[1]
    per_piece = held.shape[2] // size_block
    chunks = capacity // CHUNK
    count = count_ref[0]

    def block_copy(g):
        part = pl.ds(g * CHUNK, CHUNK)
        return pltpu.make_async_copy(blocks.at[part], held_blocks.at[part], block_sems.at[g])

    for g in range(chunks):
        @pl.when(g * CHUNK < count)
        def _(g=g):
            block_copy(g).start()

    total[...] = jnp.zeros_like(total)
    for part, held_pieces in zip(pieces, inputs):
        for n, p in enumerate(held_pieces):
            held[p] = part[n]

    def place(index):
        column = pl.multiple_of((index % per_piece) * size_block, size_block)
        return index // per_piece, slice(None), pl.ds(column, size_block)

    def group(first):
        products = []
        for n in range(0, UNROLL, 2):
            slot = first + n
            picked = jnp.concatenate([held[place(take_ref[slot])], held[place(take_ref[slot + 1])]], axis=0)
            if contract == 0:
                pair = jnp.concatenate([held_blocks[slot], held_blocks[slot + 1]], axis=1)
            else:
                pair = held_blocks[pl.ds(slot, 2)].reshape(2 * size_block, size_block)
            product = lax.dot_general(
                picked, pair, (((1,), (contract,)), ((), ())), preferred_element_type=jnp.float32
            )
            rows = product.shape[0] // 2
            products += [product[:rows, :size_block], product[rows:, size_block:]]
        for n, product in enumerate(products):
            total[place(put_ref[first + n])] += product

    @pl.loop(0, (count + CHUNK - 1) // CHUNK)
    def _(g):
        block_copy(g).wait()
        for n in range(0, CHUNK, UNROLL):
            group(g * CHUNK + n)

    for out, held_pieces in zip(outs, outputs):
        for n, p in enumerate(held_pieces):
            out[n] = total[p].astype(out.dtype)


def block_product(contract, inputs, outputs, dtypes, n_put, count, take, put, pieces, blocks):
    capacity, size_block = blocks.shape[0], blocks.shape[1]
    vector_count, own_rows = pieces[0].shape[-2:]
    pieces = [part.reshape(-1, vector_count, own_rows) for part in pieces]
    n_in = sum(part.shape[0] for part in pieces)
    smem = pl.BlockSpec(memory_space=pltpu.SMEM)
    vmem = pl.BlockSpec(memory_space=pltpu.VMEM)
    hbm = pl.BlockSpec(memory_space=pltpu.HBM)
    return pl.pallas_call(
        functools.partial(product_kernel, contract, inputs, outputs),
        out_shape=[
            jax.ShapeDtypeStruct((len(held), vector_count, own_rows), dtype) for held, dtype in zip(outputs, dtypes)
        ],
        in_specs=[smem] * 3 + [vmem] * len(pieces) + [hbm],
        out_specs=[pl.BlockSpec(memory_space=pltpu.VMEM)] * len(outputs),
        scratch_shapes=[
            pltpu.VMEM((n_in, vector_count, own_rows), jnp.bfloat16),
            pltpu.VMEM(blocks.shape, blocks.dtype),
            pltpu.VMEM((n_put + 1, vector_count, own_rows), jnp.float32),
            pltpu.SemaphoreType.DMA((capacity // CHUNK,)),
        ],
        compiler_params=pltpu.CompilerParams(vmem_limit_bytes=40 * 1024 * 1024),
        cost_estimate=pl.CostEstimate(
            flops=2 * capacity * size_block * size_block * 256,
            bytes_accessed=2 * blocks.size + 2 * n_in * vector_count * own_rows,
            transcendentals=0,
        ),
        name="mirror" if contract == 0 else "forward",
    )(count, take, put, *pieces, pltpu.with_memory_space_constraint(blocks, pltpu.HBM))


def shards(n_row, n_col, vectors, block_values, block_rows, block_cols, block_counts, center, radius):
    size_block = block_values.shape[1]
    own_rows = vectors.shape[1]
    per_piece = own_rows // size_block
    center_value = center[0]
    radius_value = radius[0]

    n_c = 2 if n_row % 2 == 0 else 1
    n_a = 4 if (n_row // n_c) % 4 == 0 else n_row // n_c
    n_b = n_row // n_c // n_a

    def at(a, b, c):
        return ((a % n_a) * n_b + b % n_b) * n_c + c % n_c

    spots = [(a, b, c) for a in range(n_a) for b in range(n_b) for c in range(n_c)]

    def shift(value, da=0, db=0, dc=0):
        pairs = [(at(a, b, c), at(a + da, b + db, c + dc)) for a, b, c in spots]
        return lax.ppermute(value, "row", pairs)

    def shift_col(value, d):
        return lax.ppermute(value, "col", [(j, (j + d) % n_col) for j in range(n_col)])

    row_index = lax.axis_index("row").astype(jnp.int32)
    col_index = lax.axis_index("col").astype(jnp.int32)
    my_c, my_b, my_a = row_index % n_c, row_index // n_c % n_b, row_index // (n_c * n_b)

    def piece(da, db, dc):
        return (dc * n_b + db) * n_a + da

    owner = block_cols // per_piece
    owner_c, owner_b, owner_a = owner % n_c, owner // n_c % n_b, owner // (n_c * n_b)
    place_cols = (
        piece((my_a - owner_a + n_a) % n_a, (my_b - owner_b + n_b) % n_b, (my_c - owner_c + n_c) % n_c) * per_piece
        + block_cols % per_piece
    )
    place_rows = (col_index - block_rows // per_piece + n_col) % n_col * per_piece + block_rows % per_piece
    live = jnp.arange(block_rows.shape[0], dtype=jnp.int32) < block_counts[0]
    put_cols = jnp.where(live, place_cols, n_row * per_piece)
    put_rows = jnp.where(live, place_rows, n_col * per_piece)

    order = list(range(1, n_a)) + [0]
    halves = [order[: n_a // 2], order[n_a // 2 :]] if n_a > 1 else [order]
    mirror_outputs = [[piece(a, b, c) for b in range(n_b) for a in order] for c in range(n_c)]
    forward_outputs = [[j] for j in range(n_col)]
    mirror_inputs = [[j] for j in range(n_col)]
    chip = [(0, b) for b in range(n_b)] + [(a, b) for b in range(n_b) for a in range(1, n_a)]
    forward_inputs = [[piece(a, b, c) for a, b in chip] for c in range(n_c)]

    def apply_operator(narrow):
        by_col = [narrow] + [shift_col(narrow, j) for j in range(1, n_col)]
        near = [narrow] + [shift(narrow, db=b) for b in range(1, n_b)]
        far = [shift(narrow, da=a) for a in range(1, n_a)]
        mirrors = block_product(
            0, mirror_inputs, mirror_outputs, [jnp.bfloat16] * len(mirror_outputs), n_row,
            block_counts, place_rows, put_cols, by_col, block_values,
        )
        by_col, far, near, mirrors = lax.optimization_barrier((by_col, far, near, mirrors))
        far_b = [shift(part, da=a) for part in near[1:] for a in range(1, n_a)]

        shares = mirrors[0].astype(jnp.float32)
        for c in range(1, n_c):
            shares += shift(mirrors[c], dc=-c).astype(jnp.float32)
        parts = []
        for b in range(n_b):
            first = b * n_a
            for half in halves:
                parts.append(shares[first : first + len(half)])
                first += len(half)
        kept = parts[: len(halves)]
        others = [
            shift(part.astype(jnp.bfloat16), db=-(n // len(halves) + 1)) for n, part in enumerate(parts[len(halves) :])
        ]
        firsts, rest = others[:: len(halves)], others[1 :: len(halves)]
        firsts, far_b = lax.optimization_barrier((firsts, far_b))


        by_chip = jnp.stack(near + far + far_b)
        by_row = [by_chip] + [shift(by_chip, dc=c) for c in range(1, n_c)]

        own = []
        back = []
        for share, received, half in zip(kept, [firsts, rest], halves):
            for other in received:
                share += other.astype(jnp.float32)
            for n, a in enumerate(half):
                if a:
                    back.append(shift(share[n].astype(jnp.bfloat16), da=-a))
                else:
                    own.append(share[n])

        forwards = block_product(
            1, forward_inputs, forward_outputs, [jnp.float32] + [jnp.bfloat16] * (n_col - 1), n_col,
            block_counts, place_cols, put_rows, by_row, block_values,
        )
        back, mine = lax.optimization_barrier((back, forwards[0]))
        forward_sum = mine[0]
        for j in range(1, n_col):
            forward_sum += shift_col(forwards[j][0], -j).astype(jnp.float32)
        mirror_sum = sum(own)
        for other in back:
            mirror_sum += other.astype(jnp.float32)
        return forward_sum + mirror_sum

    current = (apply_operator(vectors.astype(jnp.bfloat16)) - center_value * vectors) / radius_value
    return 2.0 * (apply_operator(current.astype(jnp.bfloat16)) - center_value * current) / radius_value - vectors


def solution(mesh):
    return jax.shard_map(
        functools.partial(shards, mesh.shape["row"], mesh.shape["col"]),
        mesh=mesh,
        in_specs=(
            P(None, ("row", "col")),
            P(("row", "col"), None, None),
            P(("row", "col")),
            P(("row", "col")),
            P(("row", "col")),
            P(),
            P(),
        ),
        out_specs=P(None, ("row", "col")),
        check_vma=False,
    )
```

```python
import functools

import jax
import jax.numpy as jnp
from jax import lax
from jax.experimental import pallas as pl
from jax.experimental.pallas import tpu as pltpu
from jax.sharding import PartitionSpec as P

CHUNK = 32
UNROLL = 32


def product_kernel(contract, inputs, outputs, count_ref, take_ref, put_ref, *refs):
    n_in = len(inputs)
    pieces = refs[:n_in]
    blocks = refs[n_in]
    outs = refs[n_in + 1 : n_in + 1 + len(outputs)]
    held, held_blocks, total, block_sems = refs[n_in + 1 + len(outputs) :]
    capacity, size_block = blocks.shape[0], blocks.shape[1]
    per_piece = held.shape[2] // size_block
    chunks = capacity // CHUNK
    count = count_ref[0]

    def block_copy(g):
        part = pl.ds(g * CHUNK, CHUNK)
        return pltpu.make_async_copy(blocks.at[part], held_blocks.at[part], block_sems.at[g])

    for g in range(chunks):
        @pl.when(g * CHUNK < count)
        def _(g=g):
            block_copy(g).start()

    total[...] = jnp.zeros_like(total)
    for part, held_pieces in zip(pieces, inputs):
        for n, p in enumerate(held_pieces):
            held[p] = part[n]

    def place(index):
        column = pl.multiple_of((index % per_piece) * size_block, size_block)
        return index // per_piece, slice(None), pl.ds(column, size_block)

    def group(first):
        products = []
        for n in range(0, UNROLL, 2):
            slot = first + n
            picked = jnp.concatenate([held[place(take_ref[slot])], held[place(take_ref[slot + 1])]], axis=0)
            if contract == 0:
                pair = jnp.concatenate([held_blocks[slot], held_blocks[slot + 1]], axis=1)
            else:
                pair = held_blocks[pl.ds(slot, 2)].reshape(2 * size_block, size_block)
            product = lax.dot_general(
                picked, pair, (((1,), (contract,)), ((), ())), preferred_element_type=jnp.float32
            )
            rows = product.shape[0] // 2
            products += [product[:rows, :size_block], product[rows:, size_block:]]
        for n, product in enumerate(products):
            total[place(put_ref[first + n])] += product

    @pl.loop(0, (count + CHUNK - 1) // CHUNK)
    def _(g):
        block_copy(g).wait()
        for n in range(0, CHUNK, UNROLL):
            group(g * CHUNK + n)

    for out, held_pieces in zip(outs, outputs):
        for n, p in enumerate(held_pieces):
            out[n] = total[p].astype(out.dtype)


def block_product(contract, inputs, outputs, dtypes, n_put, count, take, put, pieces, blocks):
    capacity, size_block = blocks.shape[0], blocks.shape[1]
    vector_count, own_rows = pieces[0].shape[-2:]
    pieces = [part.reshape(-1, vector_count, own_rows) for part in pieces]
    n_in = sum(part.shape[0] for part in pieces)
    smem = pl.BlockSpec(memory_space=pltpu.SMEM)
    vmem = pl.BlockSpec(memory_space=pltpu.VMEM)
    hbm = pl.BlockSpec(memory_space=pltpu.HBM)
    return pl.pallas_call(
        functools.partial(product_kernel, contract, inputs, outputs),
        out_shape=[
            jax.ShapeDtypeStruct((len(held), vector_count, own_rows), dtype) for held, dtype in zip(outputs, dtypes)
        ],
        in_specs=[smem] * 3 + [vmem] * len(pieces) + [hbm],
        out_specs=[pl.BlockSpec(memory_space=pltpu.VMEM)] * len(outputs),
        scratch_shapes=[
            pltpu.VMEM((n_in, vector_count, own_rows), jnp.bfloat16),
            pltpu.VMEM(blocks.shape, blocks.dtype),
            pltpu.VMEM((n_put + 1, vector_count, own_rows), jnp.float32),
            pltpu.SemaphoreType.DMA((capacity // CHUNK,)),
        ],
        compiler_params=pltpu.CompilerParams(vmem_limit_bytes=40 * 1024 * 1024),
        cost_estimate=pl.CostEstimate(
            flops=2 * capacity * size_block * size_block * 256,
            bytes_accessed=2 * blocks.size + 2 * n_in * vector_count * own_rows,
            transcendentals=0,
        ),
        name="mirror" if contract == 0 else "forward",
    )(count, take, put, *pieces, pltpu.with_memory_space_constraint(blocks, pltpu.HBM))


def shards(n_row, n_col, vectors, block_values, block_rows, block_cols, block_counts, center, radius):
    size_block = block_values.shape[1]
    own_rows = vectors.shape[1]
    per_piece = own_rows // size_block
    center_value = center[0]
    radius_value = radius[0]

    n_c = 2 if n_row % 2 == 0 else 1
    n_a = 4 if (n_row // n_c) % 4 == 0 else n_row // n_c
    n_b = n_row // n_c // n_a

    def at(a, b, c):
        return ((a % n_a) * n_b + b % n_b) * n_c + c % n_c

    spots = [(a, b, c) for a in range(n_a) for b in range(n_b) for c in range(n_c)]

    def shift(value, da=0, db=0, dc=0):
        pairs = [(at(a, b, c), at(a + da, b + db, c + dc)) for a, b, c in spots]
        return lax.ppermute(value, "row", pairs)

    def shift_col(value, d):
        return lax.ppermute(value, "col", [(j, (j + d) % n_col) for j in range(n_col)])

    row_index = lax.axis_index("row").astype(jnp.int32)
    col_index = lax.axis_index("col").astype(jnp.int32)
    my_c, my_b, my_a = row_index % n_c, row_index // n_c % n_b, row_index // (n_c * n_b)

    def piece(da, db, dc):
        return (dc * n_b + db) * n_a + da

    owner = block_cols // per_piece
    owner_c, owner_b, owner_a = owner % n_c, owner // n_c % n_b, owner // (n_c * n_b)
    place_cols = (
        piece((my_a - owner_a + n_a) % n_a, (my_b - owner_b + n_b) % n_b, (my_c - owner_c + n_c) % n_c) * per_piece
        + block_cols % per_piece
    )
    sum_cols = (
        piece(owner_a, (my_b - owner_b + n_b) % n_b, (my_c - owner_c + n_c) % n_c) * per_piece + block_cols % per_piece
    )
    place_rows = (col_index - block_rows // per_piece + n_col) % n_col * per_piece + block_rows % per_piece
    live = jnp.arange(block_rows.shape[0], dtype=jnp.int32) < block_counts[0]
    put_cols = jnp.where(live, sum_cols, n_row * per_piece)
    put_rows = jnp.where(live, place_rows, n_col * per_piece)

    mirror_outputs = [[piece(a, b, c) for b in range(n_b) for a in range(n_a)] for c in range(n_c)]
    forward_outputs = [[j] for j in range(n_col)]
    mirror_inputs = [[j] for j in range(n_col)]
    forward_inputs = []
    for c in range(n_c):
        forward_inputs.append([piece(0, b, c) for b in range(n_b)] + [piece(a, 0, c) for a in range(1, n_a)])
        if n_b > 1:
            forward_inputs.append([piece(a, b, c) for b in range(1, n_b) for a in range(1, n_a)])

    def apply_operator(narrow):
        by_col = [narrow] + [shift_col(narrow, j) for j in range(1, n_col)]
        near = [narrow] + [shift(narrow, db=b) for b in range(1, n_b)]
        far = [[shift(part, da=a) for a in range(1, n_a)] for part in near]
        mirrors = block_product(
            0, mirror_inputs, mirror_outputs, [jnp.bfloat16] * len(mirror_outputs), n_row,
            block_counts, place_rows, put_cols, by_col, block_values,
        )
        far[0], mirrors = lax.optimization_barrier((far[0], mirrors))

        shares = mirrors[0].astype(jnp.float32)
        for c in range(1, n_c):
            shares += shift(mirrors[c], dc=-c).astype(jnp.float32)
        by_b = [shares[b * n_a : (b + 1) * n_a] for b in range(n_b)]
        others = [shift(by_b[b].astype(jnp.bfloat16), db=-b) for b in range(1, n_b)]

        early = jnp.stack(near + far[0])
        late = [part for behind in far[1:] for part in behind]
        late = [jnp.stack(late)] if late else []
        by_row = [early] + late
        for c in range(1, n_c):
            by_row += [shift(part, dc=c) for part in [early] + late]
        by_row, others = lax.optimization_barrier((by_row, others))

        share = by_b[0]
        for other in others:
            share += other.astype(jnp.float32)
        lines = [[at(a, b, c) for a in range(n_a)] for b in range(n_b) for c in range(n_c)]
        back = lax.all_to_all(share.astype(jnp.bfloat16), "row", 0, 0, axis_index_groups=lines)

        forwards = block_product(
            1, forward_inputs, forward_outputs, [jnp.float32] + [jnp.bfloat16] * (n_col - 1), n_col,
            block_counts, place_cols, put_rows, by_row, block_values,
        )
        back, own = lax.optimization_barrier((back, forwards[0]))
        forward_sum = own[0]
        for j in range(1, n_col):
            forward_sum += shift_col(forwards[j][0], -j).astype(jnp.float32)
        mirror_sum = jnp.sum(back.astype(jnp.float32), axis=0)
        return forward_sum + mirror_sum

    current = (apply_operator(vectors.astype(jnp.bfloat16)) - center_value * vectors) / radius_value
    return 2.0 * (apply_operator(current.astype(jnp.bfloat16)) - center_value * current) / radius_value - vectors


def solution(mesh):
    return jax.shard_map(
        functools.partial(shards, mesh.shape["row"], mesh.shape["col"]),
        mesh=mesh,
        in_specs=(
            P(None, ("row", "col")),
            P(("row", "col"), None, None),
            P(("row", "col")),
            P(("row", "col")),
            P(("row", "col")),
            P(),
            P(),
        ),
        out_specs=P(None, ("row", "col")),
        check_vma=False,
    )
```

```python
import functools

import jax
import jax.numpy as jnp
from jax import lax
from jax.experimental import pallas as pl
from jax.experimental.pallas import tpu as pltpu
from jax.sharding import PartitionSpec as P

CHUNK = 32
UNROLL = 32


def product_kernel(contract, inputs, outputs, count_ref, take_ref, put_ref, *refs):
    n_in = len(inputs)
    pieces = refs[:n_in]
    blocks = refs[n_in]
    outs = refs[n_in + 1 : n_in + 1 + len(outputs)]
    held, held_blocks, total, block_sems = refs[n_in + 1 + len(outputs) :]
    capacity, size_block = blocks.shape[0], blocks.shape[1]
    per_piece = held.shape[2] // size_block
    chunks = capacity // CHUNK
    count = count_ref[0]

    def block_copy(g):
        part = pl.ds(g * CHUNK, CHUNK)
        return pltpu.make_async_copy(blocks.at[part], held_blocks.at[part], block_sems.at[g])

    for g in range(chunks):
        @pl.when(g * CHUNK < count)
        def _(g=g):
            block_copy(g).start()

    total[...] = jnp.zeros_like(total)
    for part, held_pieces in zip(pieces, inputs):
        for n, p in enumerate(held_pieces):
            held[p] = part[n]

    def place(index):
        column = pl.multiple_of((index % per_piece) * size_block, size_block)
        return index // per_piece, slice(None), pl.ds(column, size_block)

    def group(first):
        products = []
        for n in range(0, UNROLL, 2):
            slot = first + n
            picked = jnp.concatenate([held[place(take_ref[slot])], held[place(take_ref[slot + 1])]], axis=0)
            if contract == 0:
                pair = jnp.concatenate([held_blocks[slot], held_blocks[slot + 1]], axis=1)
            else:
                pair = held_blocks[pl.ds(slot, 2)].reshape(2 * size_block, size_block)
            product = lax.dot_general(
                picked, pair, (((1,), (contract,)), ((), ())), preferred_element_type=jnp.float32
            )
            rows = product.shape[0] // 2
            products += [product[:rows, :size_block], product[rows:, size_block:]]
        for n, product in enumerate(products):
            total[place(put_ref[first + n])] += product

    @pl.loop(0, (count + CHUNK - 1) // CHUNK)
    def _(g):
        block_copy(g).wait()
        for n in range(0, CHUNK, UNROLL):
            group(g * CHUNK + n)

    for out, held_pieces in zip(outs, outputs):
        for n, p in enumerate(held_pieces):
            out[n] = total[p].astype(out.dtype)


def block_product(contract, inputs, outputs, dtypes, n_put, count, take, put, pieces, blocks):
    capacity, size_block = blocks.shape[0], blocks.shape[1]
    vector_count, own_rows = pieces[0].shape[-2:]
    pieces = [part.reshape(-1, vector_count, own_rows) for part in pieces]
    n_in = sum(part.shape[0] for part in pieces)
    smem = pl.BlockSpec(memory_space=pltpu.SMEM)
    vmem = pl.BlockSpec(memory_space=pltpu.VMEM)
    hbm = pl.BlockSpec(memory_space=pltpu.HBM)
    return pl.pallas_call(
        functools.partial(product_kernel, contract, inputs, outputs),
        out_shape=[
            jax.ShapeDtypeStruct((len(held), vector_count, own_rows), dtype) for held, dtype in zip(outputs, dtypes)
        ],
        in_specs=[smem] * 3 + [vmem] * len(pieces) + [hbm],
        out_specs=[pl.BlockSpec(memory_space=pltpu.VMEM)] * len(outputs),
        scratch_shapes=[
            pltpu.VMEM((n_in, vector_count, own_rows), jnp.bfloat16),
            pltpu.VMEM(blocks.shape, blocks.dtype),
            pltpu.VMEM((n_put + 1, vector_count, own_rows), jnp.float32),
            pltpu.SemaphoreType.DMA((capacity // CHUNK,)),
        ],
        compiler_params=pltpu.CompilerParams(vmem_limit_bytes=40 * 1024 * 1024),
        cost_estimate=pl.CostEstimate(
            flops=size_block,
            bytes_accessed=size_block,
            transcendentals=0,
        ),
        name="mirror" if contract == 0 else "forward",
    )(count, take, put, *pieces, pltpu.with_memory_space_constraint(blocks, pltpu.HBM))


def shards(n_row, n_col, vectors, block_values, block_rows, block_cols, block_counts, center, radius):
    size_block = block_values.shape[1]
    own_rows = vectors.shape[1]
    per_piece = own_rows // size_block
    center_value = center[0]
    radius_value = radius[0]

    n_c = 2 if n_row % 2 == 0 else 1
    n_a = 4 if (n_row // n_c) % 4 == 0 else n_row // n_c
    n_b = n_row // n_c // n_a

    def at(a, b, c):
        return ((a % n_a) * n_b + b % n_b) * n_c + c % n_c

    spots = [(a, b, c) for a in range(n_a) for b in range(n_b) for c in range(n_c)]

    def shift(value, da=0, db=0, dc=0):
        pairs = [(at(a, b, c), at(a + da, b + db, c + dc)) for a, b, c in spots]
        return lax.ppermute(value, "row", pairs)

    def shift_col(value, d):
        return lax.ppermute(value, "col", [(j, (j + d) % n_col) for j in range(n_col)])

    row_index = lax.axis_index("row").astype(jnp.int32)
    col_index = lax.axis_index("col").astype(jnp.int32)
    my_c, my_b, my_a = row_index % n_c, row_index // n_c % n_b, row_index // (n_c * n_b)

    def piece(da, db, dc):
        return (dc * n_b + db) * n_a + da

    owner = block_cols // per_piece
    owner_c, owner_b, owner_a = owner % n_c, owner // n_c % n_b, owner // (n_c * n_b)
    place_cols = (
        piece((my_a - owner_a + n_a) % n_a, (my_b - owner_b + n_b) % n_b, (my_c - owner_c + n_c) % n_c) * per_piece
        + block_cols % per_piece
    )
    place_rows = (col_index - block_rows // per_piece + n_col) % n_col * per_piece + block_rows % per_piece
    live = jnp.arange(block_rows.shape[0], dtype=jnp.int32) < block_counts[0]
    put_cols = jnp.where(live, place_cols, n_row * per_piece)
    put_rows = jnp.where(live, place_rows, n_col * per_piece)

    order = list(range(1, n_a)) + [0]
    halves = [order]
    mirror_outputs = [[piece(a, b, c) for b in range(n_b) for a in order] for c in range(n_c)]
    forward_outputs = [[j] for j in range(n_col)]
    mirror_inputs = [[j] for j in range(n_col)]
    chip = [[(0, b) for b in range(n_b)] + [(a, 0) for a in range(1, n_a)]]
    rest_of_chip = [(a, b) for b in range(1, n_b) for a in range(1, n_a) if a != n_a // 2]
    rest_of_chip += [(n_a // 2, b) for b in range(1, n_b) if n_a > 1]
    if rest_of_chip:
        chip.append(rest_of_chip)
    forward_inputs = [[piece(a, b, c) for a, b in part] for c in range(n_c) for part in chip]

    def apply_operator(narrow):
        by_col = [narrow] + [shift_col(narrow, j) for j in range(1, n_col)]
        near = [narrow] + [shift(narrow, db=b) for b in range(1, n_b)]
        far = [shift(narrow, da=a) for a in range(1, n_a)]
        mirrors = block_product(
            0, mirror_inputs, mirror_outputs, [jnp.bfloat16] * len(mirror_outputs), n_row,
            block_counts, place_rows, put_cols, by_col, block_values,
        )
        by_col, far, near, mirrors = lax.optimization_barrier((by_col, far, near, mirrors))
        middle = n_a // 2
        across = [shift(far[middle - 1], db=b) for b in range(1, n_b)] if middle else []

        shares = mirrors[0].astype(jnp.float32)
        for c in range(1, n_c):
            shares += shift(mirrors[c], dc=-c).astype(jnp.float32)
        parts = []
        for b in range(n_b):
            first = b * n_a
            for half in halves:
                parts.append(shares[first : first + len(half)])
                first += len(half)
        kept = parts[: len(halves)]
        sends = [part.astype(jnp.bfloat16) for part in parts[len(halves) :]]
        others = [shift(send, db=-(n // len(halves) + 1)) for n, send in enumerate(sends)]
        firsts = others
        far_b = [shift(part, da=a) for part in near[1:] for a in range(1, n_a) if a != middle]
        early = jnp.stack(near + far)
        by_row = [[early] + [shift(early, dc=c) for c in range(1, n_c)]]
        if far_b + across:
            last = jnp.stack(far_b + across)
            by_row.append([last] + [shift(last, dc=c) for c in range(1, n_c)])
        by_row = [part[c] for c in range(n_c) for part in by_row]

        own = []
        back = []

        def add_up(share, received, half):
            for other in received:
                share += other.astype(jnp.float32)
            for n, a in enumerate(half):
                if a:
                    back.append(shift(share[n].astype(jnp.bfloat16), da=-a))
                else:
                    own.append(share[n])

        forwards = block_product(
            1, forward_inputs, forward_outputs, [jnp.float32] + [jnp.bfloat16] * (n_col - 1), n_col,
            block_counts, place_cols, put_rows, by_row, block_values,
        )
        firsts, mine = lax.optimization_barrier((firsts, forwards[0]))
        add_up(kept[0], firsts, halves[0])
        forward_sum = mine[0]
        for j in range(1, n_col):
            forward_sum += shift_col(forwards[j][0], -j).astype(jnp.float32)
        mirror_sum = sum(own)
        for other in back:
            mirror_sum += other.astype(jnp.float32)
        return forward_sum + mirror_sum

    current = (apply_operator(vectors.astype(jnp.bfloat16)) - center_value * vectors) / radius_value
    return 2.0 * (apply_operator(current.astype(jnp.bfloat16)) - center_value * current) / radius_value - vectors


def solution(mesh):
    return jax.shard_map(
        functools.partial(shards, mesh.shape["row"], mesh.shape["col"]),
        mesh=mesh,
        in_specs=(
            P(None, ("row", "col")),
            P(("row", "col"), None, None),
            P(("row", "col")),
            P(("row", "col")),
            P(("row", "col")),
            P(),
            P(),
        ),
        out_specs=P(None, ("row", "col")),
        check_vma=False,
    )
```

```python
import functools

import jax
import jax.numpy as jnp
from jax import lax
from jax.experimental import pallas as pl
from jax.experimental.pallas import tpu as pltpu
from jax.sharding import PartitionSpec as P

CHUNK = 32
UNROLL = 32


def product_kernel(contract, inputs, outputs, count_ref, take_ref, put_ref, *refs):
    n_in = len(inputs)
    pieces = refs[:n_in]
    blocks = refs[n_in]
    outs = refs[n_in + 1 : n_in + 1 + len(outputs)]
    held, held_blocks, total, block_sems = refs[n_in + 1 + len(outputs) :]
    capacity, size_block = blocks.shape[0], blocks.shape[1]
    per_piece = held.shape[2] // size_block
    chunks = capacity // CHUNK
    count = count_ref[0]

    def block_copy(g):
        part = pl.ds(g * CHUNK, CHUNK)
        return pltpu.make_async_copy(blocks.at[part], held_blocks.at[part], block_sems.at[g])

    for g in range(chunks):
        @pl.when(g * CHUNK < count)
        def _(g=g):
            block_copy(g).start()

    total[...] = jnp.zeros_like(total)
    for part, held_pieces in zip(pieces, inputs):
        for n, p in enumerate(held_pieces):
            held[p] = part[n]

    def place(index):
        column = pl.multiple_of((index % per_piece) * size_block, size_block)
        return index // per_piece, slice(None), pl.ds(column, size_block)

    def group(first):
        products = []
        for n in range(0, UNROLL, 2):
            slot = first + n
            picked = jnp.concatenate([held[place(take_ref[slot])], held[place(take_ref[slot + 1])]], axis=0)
            if contract == 0:
                pair = jnp.concatenate([held_blocks[slot], held_blocks[slot + 1]], axis=1)
            else:
                pair = held_blocks[pl.ds(slot, 2)].reshape(2 * size_block, size_block)
            product = lax.dot_general(
                picked, pair, (((1,), (contract,)), ((), ())), preferred_element_type=jnp.float32
            )
            rows = product.shape[0] // 2
            products += [product[:rows, :size_block], product[rows:, size_block:]]
        for n, product in enumerate(products):
            total[place(put_ref[first + n])] += product

    @pl.loop(0, (count + CHUNK - 1) // CHUNK)
    def _(g):
        block_copy(g).wait()
        for n in range(0, CHUNK, UNROLL):
            group(g * CHUNK + n)

    for out, held_pieces in zip(outs, outputs):
        for n, p in enumerate(held_pieces):
            out[n] = total[p].astype(out.dtype)


def block_product(contract, inputs, outputs, dtypes, n_put, count, take, put, pieces, blocks):
    capacity, size_block = blocks.shape[0], blocks.shape[1]
    vector_count, own_rows = pieces[0].shape[-2:]
    pieces = [part.reshape(-1, vector_count, own_rows) for part in pieces]
    n_in = sum(part.shape[0] for part in pieces)
    smem = pl.BlockSpec(memory_space=pltpu.SMEM)
    vmem = pl.BlockSpec(memory_space=pltpu.VMEM)
    hbm = pl.BlockSpec(memory_space=pltpu.HBM)
    return pl.pallas_call(
        functools.partial(product_kernel, contract, inputs, outputs),
        out_shape=[
            jax.ShapeDtypeStruct((len(held), vector_count, own_rows), dtype) for held, dtype in zip(outputs, dtypes)
        ],
        in_specs=[smem] * 3 + [vmem] * len(pieces) + [hbm],
        out_specs=[pl.BlockSpec(memory_space=pltpu.VMEM)] * len(outputs),
        scratch_shapes=[
            pltpu.VMEM((n_in, vector_count, own_rows), jnp.bfloat16),
            pltpu.VMEM(blocks.shape, blocks.dtype),
            pltpu.VMEM((n_put + 1, vector_count, own_rows), jnp.float32),
            pltpu.SemaphoreType.DMA((capacity // CHUNK,)),
        ],
        compiler_params=pltpu.CompilerParams(vmem_limit_bytes=40 * 1024 * 1024),
        cost_estimate=pl.CostEstimate(
            flops=size_block,
            bytes_accessed=size_block,
            transcendentals=0,
        ),
        name="mirror" if contract == 0 else "forward",
    )(count, take, put, *pieces, pltpu.with_memory_space_constraint(blocks, pltpu.HBM))


def shards(n_row, n_col, vectors, block_values, block_rows, block_cols, block_counts, center, radius):
    size_block = block_values.shape[1]
    own_rows = vectors.shape[1]
    per_piece = own_rows // size_block
    center_value = center[0]
    radius_value = radius[0]

    n_c = 2 if n_row % 2 == 0 else 1
    n_a = 4 if (n_row // n_c) % 4 == 0 else n_row // n_c
    n_b = n_row // n_c // n_a

    def at(a, b, c):
        return ((a % n_a) * n_b + b % n_b) * n_c + c % n_c

    spots = [(a, b, c) for a in range(n_a) for b in range(n_b) for c in range(n_c)]

    def shift(value, da=0, db=0, dc=0):
        pairs = [(at(a, b, c), at(a + da, b + db, c + dc)) for a, b, c in spots]
        return lax.ppermute(value, "row", pairs)

    def shift_col(value, d):
        return lax.ppermute(value, "col", [(j, (j + d) % n_col) for j in range(n_col)])

    row_index = lax.axis_index("row").astype(jnp.int32)
    col_index = lax.axis_index("col").astype(jnp.int32)
    my_c, my_b, my_a = row_index % n_c, row_index // n_c % n_b, row_index // (n_c * n_b)

    def piece(da, db, dc):
        return (dc * n_b + db) * n_a + da

    owner = block_cols // per_piece
    owner_c, owner_b, owner_a = owner % n_c, owner // n_c % n_b, owner // (n_c * n_b)
    place_cols = (
        piece((my_a - owner_a + n_a) % n_a, (my_b - owner_b + n_b) % n_b, (my_c - owner_c + n_c) % n_c) * per_piece
        + block_cols % per_piece
    )
    place_rows = (col_index - block_rows // per_piece + n_col) % n_col * per_piece + block_rows % per_piece
    live = jnp.arange(block_rows.shape[0], dtype=jnp.int32) < block_counts[0]
    put_cols = jnp.where(live, place_cols, n_row * per_piece)
    put_rows = jnp.where(live, place_rows, n_col * per_piece)

    order = list(range(1, n_a)) + [0]
    halves = [order]
    mirror_outputs = [[piece(a, b, c) for b in range(n_b) for a in order] for c in range(n_c)]
    forward_outputs = [[j] for j in range(n_col)]
    mirror_inputs = [[j] for j in range(n_col)]
    chip = [[(0, b) for b in range(n_b)] + [(a, 0) for a in range(1, n_a)]]
    rest_of_chip = [(a, b) for b in range(1, n_b) for a in range(1, n_a) if a != n_a // 2]
    rest_of_chip += [(n_a // 2, b) for b in range(1, n_b) if n_a > 1]
    if rest_of_chip:
        chip.append(rest_of_chip)
    forward_inputs = [[piece(a, b, c) for a, b in part] for c in range(n_c) for part in chip]

    def apply_operator(narrow):
        by_col = [narrow] + [shift_col(narrow, j) for j in range(1, n_col)]
        near = [narrow] + [shift(narrow, db=b) for b in range(1, n_b)]
        far = [shift(narrow, da=a) for a in range(1, n_a)]
        mirrors = block_product(
            0, mirror_inputs, mirror_outputs, [jnp.bfloat16] * len(mirror_outputs), n_row,
            block_counts, place_rows, put_cols, by_col, block_values,
        )
        mirrors = list(mirrors)
        far, mirrors[0] = lax.optimization_barrier((far, mirrors[0]))
        middle = n_a // 2
        across = [shift(far[middle - 1], db=b) for b in range(1, n_b)] if middle else []

        shares = mirrors[0].astype(jnp.float32)
        for c in range(1, n_c):
            shares += shift(mirrors[c], dc=-c).astype(jnp.float32)
        parts = []
        for b in range(n_b):
            first = b * n_a
            for half in halves:
                parts.append(shares[first : first + len(half)])
                first += len(half)
        kept = parts[: len(halves)]
        sends = [part.astype(jnp.bfloat16) for part in parts[len(halves) :]]
        others = [shift(send, db=-(n // len(halves) + 1)) for n, send in enumerate(sends)]
        firsts = others
        far_b = [shift(part, da=a) for part in near[1:] for a in range(1, n_a) if a != middle]
        early = jnp.stack(near + far)
        by_row = [[early] + [shift(early, dc=c) for c in range(1, n_c)]]
        if far_b + across:
            last = jnp.stack(far_b + across)
            by_row.append([last] + [shift(last, dc=c) for c in range(1, n_c)])
        by_row = [part[c] for c in range(n_c) for part in by_row]

        own = []
        back = []

        def add_up(share, received, half):
            for other in received:
                share += other.astype(jnp.float32)
            for n, a in enumerate(half):
                if a:
                    back.append(shift(share[n].astype(jnp.bfloat16), da=-a))
                else:
                    own.append(share[n])

        forwards = block_product(
            1, forward_inputs, forward_outputs, [jnp.float32] + [jnp.bfloat16] * (n_col - 1), n_col,
            block_counts, place_cols, put_rows, by_row, block_values,
        )
        firsts, mine = lax.optimization_barrier((firsts, forwards[0]))
        add_up(kept[0], firsts, halves[0])
        forward_sum = mine[0]
        for j in range(1, n_col):
            forward_sum += shift_col(forwards[j][0], -j).astype(jnp.float32)
        mirror_sum = sum(own)
        for other in back:
            mirror_sum += other.astype(jnp.float32)
        return forward_sum + mirror_sum

    current = (apply_operator(vectors.astype(jnp.bfloat16)) - center_value * vectors) / radius_value
    return 2.0 * (apply_operator(current.astype(jnp.bfloat16)) - center_value * current) / radius_value - vectors


def solution(mesh):
    return jax.shard_map(
        functools.partial(shards, mesh.shape["row"], mesh.shape["col"]),
        mesh=mesh,
        in_specs=(
            P(None, ("row", "col")),
            P(("row", "col"), None, None),
            P(("row", "col")),
            P(("row", "col")),
            P(("row", "col")),
            P(),
            P(),
        ),
        out_specs=P(None, ("row", "col")),
        check_vma=False,
    )
```

```python
import functools

import jax
import jax.numpy as jnp
from jax import lax
from jax.experimental import pallas as pl
from jax.experimental.pallas import tpu as pltpu
from jax.sharding import PartitionSpec as P

CHUNK = 32
UNROLL = 32


def product_kernel(contract, inputs, outputs, count_ref, take_ref, put_ref, *refs):
    n_in = len(inputs)
    pieces = refs[:n_in]
    blocks = refs[n_in]
    outs = refs[n_in + 1 : n_in + 1 + len(outputs)]
    held, held_blocks, total, block_sems = refs[n_in + 1 + len(outputs) :]
    capacity, size_block = blocks.shape[0], blocks.shape[1]
    per_piece = held.shape[2] // size_block
    chunks = capacity // CHUNK
    count = count_ref[0]

    def block_copy(g):
        part = pl.ds(g * CHUNK, CHUNK)
        return pltpu.make_async_copy(blocks.at[part], held_blocks.at[part], block_sems.at[g])

    for g in range(chunks):
        @pl.when(g * CHUNK < count)
        def _(g=g):
            block_copy(g).start()

    total[...] = jnp.zeros_like(total)
    for part, held_pieces in zip(pieces, inputs):
        for n, p in enumerate(held_pieces):
            held[p] = part[n]

    def place(index):
        column = pl.multiple_of((index % per_piece) * size_block, size_block)
        return index // per_piece, slice(None), pl.ds(column, size_block)

    def group(first):
        products = []
        for n in range(0, UNROLL, 2):
            slot = first + n
            picked = jnp.concatenate([held[place(take_ref[slot])], held[place(take_ref[slot + 1])]], axis=0)
            if contract == 0:
                pair = jnp.concatenate([held_blocks[slot], held_blocks[slot + 1]], axis=1)
            else:
                pair = held_blocks[pl.ds(slot, 2)].reshape(2 * size_block, size_block)
            product = lax.dot_general(
                picked, pair, (((1,), (contract,)), ((), ())), preferred_element_type=jnp.float32
            )
            rows = product.shape[0] // 2
            products += [product[:rows, :size_block], product[rows:, size_block:]]
        for n, product in enumerate(products):
            total[place(put_ref[first + n])] += product

    @pl.loop(0, (count + CHUNK - 1) // CHUNK)
    def _(g):
        block_copy(g).wait()
        for n in range(0, CHUNK, UNROLL):
            group(g * CHUNK + n)

    for out, held_pieces in zip(outs, outputs):
        for n, p in enumerate(held_pieces):
            out[n] = total[p].astype(out.dtype)


def block_product(contract, inputs, outputs, dtypes, n_put, count, take, put, pieces, blocks):
    capacity, size_block = blocks.shape[0], blocks.shape[1]
    vector_count, own_rows = pieces[0].shape[-2:]
    pieces = [part.reshape(-1, vector_count, own_rows) for part in pieces]
    n_in = sum(part.shape[0] for part in pieces)
    smem = pl.BlockSpec(memory_space=pltpu.SMEM)
    vmem = pl.BlockSpec(memory_space=pltpu.VMEM)
    hbm = pl.BlockSpec(memory_space=pltpu.HBM)
    return pl.pallas_call(
        functools.partial(product_kernel, contract, inputs, outputs),
        out_shape=[
            jax.ShapeDtypeStruct((len(held), vector_count, own_rows), dtype) for held, dtype in zip(outputs, dtypes)
        ],
        in_specs=[smem] * 3 + [vmem] * len(pieces) + [hbm],
        out_specs=[pl.BlockSpec(memory_space=pltpu.VMEM)] * len(outputs),
        scratch_shapes=[
            pltpu.VMEM((n_in, vector_count, own_rows), jnp.bfloat16),
            pltpu.VMEM(blocks.shape, blocks.dtype),
            pltpu.VMEM((n_put + 1, vector_count, own_rows), jnp.float32),
            pltpu.SemaphoreType.DMA((capacity // CHUNK,)),
        ],
        compiler_params=pltpu.CompilerParams(vmem_limit_bytes=40 * 1024 * 1024),
        cost_estimate=pl.CostEstimate(
            flops=size_block,
            bytes_accessed=size_block,
            transcendentals=0,
        ),
        name="mirror" if contract == 0 else "forward",
    )(count, take, put, *pieces, pltpu.with_memory_space_constraint(blocks, pltpu.HBM))


def shards(n_row, n_col, vectors, block_values, block_rows, block_cols, block_counts, center, radius):
    size_block = block_values.shape[1]
    own_rows = vectors.shape[1]
    per_piece = own_rows // size_block
    center_value = center[0]
    radius_value = radius[0]

    n_c = 2 if n_row % 2 == 0 else 1
    n_a = 4 if (n_row // n_c) % 4 == 0 else n_row // n_c
    n_b = n_row // n_c // n_a

    def at(a, b, c):
        return ((a % n_a) * n_b + b % n_b) * n_c + c % n_c

    spots = [(a, b, c) for a in range(n_a) for b in range(n_b) for c in range(n_c)]

    def shift(value, da=0, db=0, dc=0):
        pairs = [(at(a, b, c), at(a + da, b + db, c + dc)) for a, b, c in spots]
        return lax.ppermute(value, "row", pairs)

    def shift_col(value, d):
        return lax.ppermute(value, "col", [(j, (j + d) % n_col) for j in range(n_col)])

    row_index = lax.axis_index("row").astype(jnp.int32)
    col_index = lax.axis_index("col").astype(jnp.int32)
    my_c, my_b, my_a = row_index % n_c, row_index // n_c % n_b, row_index // (n_c * n_b)

    def piece(da, db, dc):
        return (dc * n_b + db) * n_a + da

    owner = block_cols // per_piece
    owner_c, owner_b, owner_a = owner % n_c, owner // n_c % n_b, owner // (n_c * n_b)
    place_cols = (
        piece((my_a - owner_a + n_a) % n_a, (my_b - owner_b + n_b) % n_b, (my_c - owner_c + n_c) % n_c) * per_piece
        + block_cols % per_piece
    )
    place_rows = (col_index - block_rows // per_piece + n_col) % n_col * per_piece + block_rows % per_piece
    live = jnp.arange(block_rows.shape[0], dtype=jnp.int32) < block_counts[0]
    put_cols = jnp.where(live, place_cols, n_row * per_piece)
    put_rows = jnp.where(live, place_rows, n_col * per_piece)

    order = list(range(1, n_a)) + [0]
    halves = [order[: n_a // 2], order[n_a // 2 :]] if n_a > 1 else [order]
    mirror_outputs = [[piece(a, b, c) for b in range(n_b) for a in order] for c in range(n_c)]
    forward_outputs = [[j] for j in range(n_col)]
    mirror_inputs = [[j] for j in range(n_col)]
    chip = [[(0, b) for b in range(n_b)] + [(a, 0) for a in range(1, n_a)]]
    rest_of_chip = [(a, b) for b in range(1, n_b) for a in range(1, n_a) if a != n_a // 2]
    rest_of_chip += [(n_a // 2, b) for b in range(1, n_b) if n_a > 1]
    if rest_of_chip:
        chip.append(rest_of_chip)
    forward_inputs = [[piece(a, b, c) for a, b in part] for c in range(n_c) for part in chip]

    def apply_operator(narrow):
        by_col = [narrow] + [shift_col(narrow, j) for j in range(1, n_col)]
        near = [narrow] + [shift(narrow, db=b) for b in range(1, n_b)]
        far = [shift(narrow, da=a) for a in range(1, n_a)]
        mirrors = block_product(
            0, mirror_inputs, mirror_outputs, [jnp.bfloat16] * len(mirror_outputs), n_row,
            block_counts, place_rows, put_cols, by_col, block_values,
        )
        mirrors = list(mirrors)
        far, mirrors[0] = lax.optimization_barrier((far, mirrors[0]))
        middle = n_a // 2
        across = [shift(far[middle - 1], db=b) for b in range(1, n_b)] if middle else []

        shares = mirrors[0].astype(jnp.float32)
        for c in range(1, n_c):
            shares += shift(mirrors[c], dc=-c).astype(jnp.float32)
        parts = []
        for b in range(n_b):
            first = b * n_a
            for half in halves:
                parts.append(shares[first : first + len(half)])
                first += len(half)
        kept = parts[: len(halves)]
        sends = [part.astype(jnp.bfloat16) for part in parts[len(halves) :]]
        others = [shift(send, db=-(n // len(halves) + 1)) for n, send in enumerate(sends)]
        firsts, rest = others[:: len(halves)], others[1 :: len(halves)]
        far_b = [shift(part, da=a) for part in near[1:] for a in range(1, n_a) if a != middle]
        far_b, across, firsts = lax.optimization_barrier((far_b, across, firsts))
        early = jnp.stack(near + far)
        by_row = [[early] + [shift(early, dc=c) for c in range(1, n_c)]]
        if far_b + across:
            last = jnp.stack(far_b + across)
            by_row.append([last] + [shift(last, dc=c) for c in range(1, n_c)])
        by_row = [part[c] for c in range(n_c) for part in by_row]

        own = []
        back = []

        def add_up(share, received, half):
            for other in received:
                share += other.astype(jnp.float32)
            for n, a in enumerate(half):
                if a:
                    back.append(shift(share[n].astype(jnp.bfloat16), da=-a))
                else:
                    own.append(share[n])

        add_up(kept[0], firsts, halves[0])
        forwards = block_product(
            1, forward_inputs, forward_outputs, [jnp.float32] + [jnp.bfloat16] * (n_col - 1), n_col,
            block_counts, place_cols, put_rows, by_row, block_values,
        )
        rest, back[:], mine = lax.optimization_barrier((rest, back, forwards[0]))
        sent = len(back)
        if len(halves) > 1:
            add_up(kept[1], rest, halves[1])
        crossed = [shift_col(forwards[j][0], -j) for j in range(1, n_col)]
        crossed, back[:sent] = lax.optimization_barrier((crossed, back[:sent]))
        forward_sum = mine[0]
        for other in crossed:
            forward_sum += other.astype(jnp.float32)
        mirror_sum = sum(own)
        for other in back:
            mirror_sum += other.astype(jnp.float32)
        return forward_sum + mirror_sum

    current = (apply_operator(vectors.astype(jnp.bfloat16)) - center_value * vectors) / radius_value
    return 2.0 * (apply_operator(current.astype(jnp.bfloat16)) - center_value * current) / radius_value - vectors


def solution(mesh):
    return jax.shard_map(
        functools.partial(shards, mesh.shape["row"], mesh.shape["col"]),
        mesh=mesh,
        in_specs=(
            P(None, ("row", "col")),
            P(("row", "col"), None, None),
            P(("row", "col")),
            P(("row", "col")),
            P(("row", "col")),
            P(),
            P(),
        ),
        out_specs=P(None, ("row", "col")),
        check_vma=False,
    )
```

```python
import functools

import jax
import jax.numpy as jnp
from jax import lax
from jax.experimental import pallas as pl
from jax.experimental.pallas import tpu as pltpu
from jax.sharding import PartitionSpec as P

CHUNK = 32
UNROLL = 64


def product_kernel(contract, inputs, outputs, count_ref, take_ref, put_ref, *refs):
    n_in = len(inputs)
    pieces = refs[:n_in]
    blocks = refs[n_in]
    outs = refs[n_in + 1 : n_in + 1 + len(outputs)]
    held, held_blocks, total, block_sems = refs[n_in + 1 + len(outputs) :]
    capacity, size_block = blocks.shape[0], blocks.shape[1]
    per_piece = held.shape[2] // size_block
    chunks = capacity // CHUNK
    count = count_ref[0]

    def block_copy(g):
        part = pl.ds(g * CHUNK, CHUNK)
        return pltpu.make_async_copy(blocks.at[part], held_blocks.at[part], block_sems.at[g])

    for g in range(chunks):
        @pl.when(g * CHUNK // UNROLL * UNROLL < count)
        def _(g=g):
            block_copy(g).start()

    total[...] = jnp.zeros_like(total)
    for part, held_pieces in zip(pieces, inputs):
        for n, p in enumerate(held_pieces):
            held[p] = part[n]

    def place(index):
        column = pl.multiple_of((index % per_piece) * size_block, size_block)
        return index // per_piece, slice(None), pl.ds(column, size_block)

    def group(first):
        products = []
        for n in range(0, UNROLL, 2):
            slot = first + n
            picked = jnp.concatenate([held[place(take_ref[slot])], held[place(take_ref[slot + 1])]], axis=0)
            if contract == 0:
                pair = jnp.concatenate([held_blocks[slot], held_blocks[slot + 1]], axis=1)
            else:
                pair = held_blocks[pl.ds(slot, 2)].reshape(2 * size_block, size_block)
            product = lax.dot_general(
                picked, pair, (((1,), (contract,)), ((), ())), preferred_element_type=jnp.float32
            )
            rows = product.shape[0] // 2
            products += [product[:rows, :size_block], product[rows:, size_block:]]
        for n, product in enumerate(products):
            total[place(put_ref[first + n])] += product

    @pl.loop(0, (count + UNROLL - 1) // UNROLL)
    def _(g):
        for n in range(UNROLL // CHUNK):
            block_copy(g * (UNROLL // CHUNK) + n).wait()
        group(g * UNROLL)

    for out, held_pieces in zip(outs, outputs):
        for n, p in enumerate(held_pieces):
            out[n] = total[p].astype(out.dtype)


def block_product(contract, inputs, outputs, dtypes, n_put, count, take, put, pieces, blocks):
    capacity, size_block = blocks.shape[0], blocks.shape[1]
    vector_count, own_rows = pieces[0].shape[-2:]
    pieces = [part.reshape(-1, vector_count, own_rows) for part in pieces]
    n_in = sum(part.shape[0] for part in pieces)
    smem = pl.BlockSpec(memory_space=pltpu.SMEM)
    vmem = pl.BlockSpec(memory_space=pltpu.VMEM)
    hbm = pl.BlockSpec(memory_space=pltpu.HBM)
    return pl.pallas_call(
        functools.partial(product_kernel, contract, inputs, outputs),
        out_shape=[
            jax.ShapeDtypeStruct((len(held), vector_count, own_rows), dtype) for held, dtype in zip(outputs, dtypes)
        ],
        in_specs=[smem] * 3 + [vmem] * len(pieces) + [hbm],
        out_specs=[pl.BlockSpec(memory_space=pltpu.VMEM)] * len(outputs),
        scratch_shapes=[
            pltpu.VMEM((n_in, vector_count, own_rows), jnp.bfloat16),
            pltpu.VMEM(blocks.shape, blocks.dtype),
            pltpu.VMEM((n_put + 1, vector_count, own_rows), jnp.float32),
            pltpu.SemaphoreType.DMA((capacity // CHUNK,)),
        ],
        compiler_params=pltpu.CompilerParams(vmem_limit_bytes=40 * 1024 * 1024),
        cost_estimate=pl.CostEstimate(
            flops=size_block,
            bytes_accessed=size_block,
            transcendentals=0,
        ),
        name="mirror" if contract == 0 else "forward",
    )(count, take, put, *pieces, pltpu.with_memory_space_constraint(blocks, pltpu.HBM))


def shards(n_row, n_col, vectors, block_values, block_rows, block_cols, block_counts, center, radius):
    size_block = block_values.shape[1]
    own_rows = vectors.shape[1]
    per_piece = own_rows // size_block
    center_value = center[0]
    radius_value = radius[0]

    n_c = 2 if n_row % 2 == 0 else 1
    n_a = 4 if (n_row // n_c) % 4 == 0 else n_row // n_c
    n_b = n_row // n_c // n_a

    def at(a, b, c):
        return ((a % n_a) * n_b + b % n_b) * n_c + c % n_c

    spots = [(a, b, c) for a in range(n_a) for b in range(n_b) for c in range(n_c)]

    def shift(value, da=0, db=0, dc=0):
        pairs = [(at(a, b, c), at(a + da, b + db, c + dc)) for a, b, c in spots]
        return lax.ppermute(value, "row", pairs)

    def shift_col(value, d):
        return lax.ppermute(value, "col", [(j, (j + d) % n_col) for j in range(n_col)])

    row_index = lax.axis_index("row").astype(jnp.int32)
    col_index = lax.axis_index("col").astype(jnp.int32)
    my_c, my_b, my_a = row_index % n_c, row_index // n_c % n_b, row_index // (n_c * n_b)

    def piece(da, db, dc):
        return (dc * n_b + db) * n_a + da

    owner = block_cols // per_piece
    owner_c, owner_b, owner_a = owner % n_c, owner // n_c % n_b, owner // (n_c * n_b)
    place_cols = (
        piece((my_a - owner_a + n_a) % n_a, (my_b - owner_b + n_b) % n_b, (my_c - owner_c + n_c) % n_c) * per_piece
        + block_cols % per_piece
    )
    place_rows = (col_index - block_rows // per_piece + n_col) % n_col * per_piece + block_rows % per_piece
    live = jnp.arange(block_rows.shape[0], dtype=jnp.int32) < block_counts[0]
    put_cols = jnp.where(live, place_cols, n_row * per_piece)
    put_rows = jnp.where(live, place_rows, n_col * per_piece)

    order = list(range(1, n_a)) + [0]
    halves = [order[:-1], order[-1:]] if n_a > 1 else [order]
    mirror_outputs = [[piece(a, b, c) for b in range(n_b) for a in order] for c in range(n_c)]
    forward_outputs = [[j] for j in range(n_col)]
    mirror_inputs = [[j] for j in range(n_col)]
    chip = [[(0, b) for b in range(n_b)] + [(a, 0) for a in range(1, n_a)]]
    rest_of_chip = [(a, b) for b in range(1, n_b) for a in range(1, n_a) if a != n_a // 2]
    rest_of_chip += [(n_a // 2, b) for b in range(1, n_b) if n_a > 1]
    if rest_of_chip:
        chip.append(rest_of_chip)
    forward_inputs = [[piece(a, b, c) for a, b in part] for c in range(n_c) for part in chip]

    def apply_operator(narrow):
        by_col = [narrow] + [shift_col(narrow, j) for j in range(1, n_col)]
        near = [narrow] + [shift(narrow, db=b) for b in range(1, n_b)]
        far = [shift(narrow, da=a) for a in range(1, n_a)]
        mirrors = block_product(
            0, mirror_inputs, mirror_outputs, [jnp.bfloat16] * len(mirror_outputs), n_row,
            block_counts, place_rows, put_cols, by_col, block_values,
        )
        mirrors = list(mirrors)
        far, mirrors[0] = lax.optimization_barrier((far, mirrors[0]))
        middle = n_a // 2
        across = [shift(far[middle - 1], db=b) for b in range(1, n_b)] if middle else []

        shares = mirrors[0].astype(jnp.float32)
        for c in range(1, n_c):
            shares += shift(mirrors[c], dc=-c).astype(jnp.float32)
        parts = []
        for b in range(n_b):
            first = b * n_a
            for half in halves:
                parts.append(shares[first : first + len(half)])
                first += len(half)
        kept = parts[: len(halves)]
        sends = [part.astype(jnp.bfloat16) for part in parts[len(halves) :]]
        others = [shift(send, db=-(n // len(halves) + 1)) for n, send in enumerate(sends)]
        firsts, rest = others[:: len(halves)], others[1 :: len(halves)]
        far_b = [shift(part, da=a) for part in near[1:] for a in range(1, n_a) if a != middle]
        far_b, across, firsts = lax.optimization_barrier((far_b, across, firsts))
        early = jnp.stack(near + far)
        by_row = [[early] + [shift(early, dc=c) for c in range(1, n_c)]]
        if far_b + across:
            last = jnp.stack(far_b + across)
            by_row.append([last] + [shift(last, dc=c) for c in range(1, n_c)])
        by_row = [part[c] for c in range(n_c) for part in by_row]

        own = []
        back = []

        def add_up(share, received, half):
            for other in received:
                share += other.astype(jnp.float32)
            for n, a in enumerate(half):
                if a:
                    back.append(shift(share[n].astype(jnp.bfloat16), da=-a))
                else:
                    own.append(share[n])

        add_up(kept[0], firsts, halves[0])
        forwards = block_product(
            1, forward_inputs, forward_outputs, [jnp.float32] + [jnp.bfloat16] * (n_col - 1), n_col,
            block_counts, place_cols, put_rows, by_row, block_values,
        )
        rest, back[:], mine = lax.optimization_barrier((rest, back, forwards[0]))
        sent = len(back)
        if len(halves) > 1:
            add_up(kept[1], rest, halves[1])
        crossed = [shift_col(forwards[j][0], -j) for j in range(1, n_col)]
        crossed, back[:sent] = lax.optimization_barrier((crossed, back[:sent]))
        forward_sum = mine[0]
        for other in crossed:
            forward_sum += other.astype(jnp.float32)
        mirror_sum = sum(own)
        for other in back:
            mirror_sum += other.astype(jnp.float32)
        return forward_sum + mirror_sum

    current = (apply_operator(vectors.astype(jnp.bfloat16)) - center_value * vectors) / radius_value
    return 2.0 * (apply_operator(current.astype(jnp.bfloat16)) - center_value * current) / radius_value - vectors


def solution(mesh):
    return jax.shard_map(
        functools.partial(shards, mesh.shape["row"], mesh.shape["col"]),
        mesh=mesh,
        in_specs=(
            P(None, ("row", "col")),
            P(("row", "col"), None, None),
            P(("row", "col")),
            P(("row", "col")),
            P(("row", "col")),
            P(),
            P(),
        ),
        out_specs=P(None, ("row", "col")),
        check_vma=False,
    )
```

```python
import functools

import jax
import jax.numpy as jnp
from jax import lax
from jax.experimental import pallas as pl
from jax.experimental.pallas import tpu as pltpu
from jax.sharding import PartitionSpec as P

CHUNK = 32
UNROLL = 64


def product_kernel(contract, inputs, outputs, count_ref, take_ref, put_ref, *refs):
    n_in = len(inputs)
    pieces = refs[:n_in]
    blocks = refs[n_in]
    outs = refs[n_in + 1 : n_in + 1 + len(outputs)]
    held, held_blocks, total, block_sems = refs[n_in + 1 + len(outputs) :]
    capacity, size_block = blocks.shape[0], blocks.shape[1]
    per_piece = held.shape[2] // size_block
    chunks = capacity // CHUNK
    count = count_ref[0]

    def block_copy(g):
        part = pl.ds(g * CHUNK, CHUNK)
        return pltpu.make_async_copy(blocks.at[part], held_blocks.at[part], block_sems.at[g])

    for g in range(chunks):
        @pl.when(g * CHUNK // UNROLL * UNROLL < count)
        def _(g=g):
            block_copy(g).start()

    total[...] = jnp.zeros_like(total)
    for part, held_pieces in zip(pieces, inputs):
        for n, p in enumerate(held_pieces):
            held[p] = part[n]

    def place(index):
        column = pl.multiple_of((index % per_piece) * size_block, size_block)
        return index // per_piece, slice(None), pl.ds(column, size_block)

    def group(first):
        products = []
        for n in range(0, UNROLL, 2):
            slot = first + n
            picked = jnp.concatenate([held[place(take_ref[slot])], held[place(take_ref[slot + 1])]], axis=0)
            if contract == 0:
                pair = jnp.concatenate([held_blocks[slot], held_blocks[slot + 1]], axis=1)
            else:
                pair = held_blocks[pl.ds(slot, 2)].reshape(2 * size_block, size_block)
            product = lax.dot_general(
                picked, pair, (((1,), (contract,)), ((), ())), preferred_element_type=jnp.float32
            )
            rows = product.shape[0] // 2
            products += [product[:rows, :size_block], product[rows:, size_block:]]
        for n, product in enumerate(products):
            total[place(put_ref[first + n])] += product

    @pl.loop(0, (count + UNROLL - 1) // UNROLL)
    def _(g):
        for n in range(UNROLL // CHUNK):
            block_copy(g * (UNROLL // CHUNK) + n).wait()
        group(g * UNROLL)

    for out, held_pieces in zip(outs, outputs):
        for n, p in enumerate(held_pieces):
            out[n] = total[p].astype(out.dtype)


def block_product(contract, inputs, outputs, dtypes, n_put, count, take, put, pieces, blocks):
    capacity, size_block = blocks.shape[0], blocks.shape[1]
    vector_count, own_rows = pieces[0].shape[-2:]
    pieces = [part.reshape(-1, vector_count, own_rows) for part in pieces]
    n_in = sum(part.shape[0] for part in pieces)
    smem = pl.BlockSpec(memory_space=pltpu.SMEM)
    vmem = pl.BlockSpec(memory_space=pltpu.VMEM)
    hbm = pl.BlockSpec(memory_space=pltpu.HBM)
    return pl.pallas_call(
        functools.partial(product_kernel, contract, inputs, outputs),
        out_shape=[
            jax.ShapeDtypeStruct((len(held), vector_count, own_rows), dtype) for held, dtype in zip(outputs, dtypes)
        ],
        in_specs=[smem] * 3 + [vmem] * len(pieces) + [hbm],
        out_specs=[pl.BlockSpec(memory_space=pltpu.VMEM)] * len(outputs),
        scratch_shapes=[
            pltpu.VMEM((n_in, vector_count, own_rows), jnp.bfloat16),
            pltpu.VMEM(blocks.shape, blocks.dtype),
            pltpu.VMEM((n_put + 1, vector_count, own_rows), jnp.float32),
            pltpu.SemaphoreType.DMA((capacity // CHUNK,)),
        ],
        compiler_params=pltpu.CompilerParams(vmem_limit_bytes=40 * 1024 * 1024),
        cost_estimate=pl.CostEstimate(
            flops=size_block,
            bytes_accessed=size_block,
            transcendentals=0,
        ),
        name="mirror" if contract == 0 else "forward",
    )(count, take, put, *pieces, pltpu.with_memory_space_constraint(blocks, pltpu.HBM))


def shards(n_row, n_col, vectors, block_values, block_rows, block_cols, block_counts, center, radius):
    size_block = block_values.shape[1]
    own_rows = vectors.shape[1]
    per_piece = own_rows // size_block
    center_value = center[0]
    radius_value = radius[0]

    n_c = 2 if n_row % 2 == 0 else 1
    n_a = 4 if (n_row // n_c) % 4 == 0 else n_row // n_c
    n_b = n_row // n_c // n_a

    def at(a, b, c):
        return ((a % n_a) * n_b + b % n_b) * n_c + c % n_c

    spots = [(a, b, c) for a in range(n_a) for b in range(n_b) for c in range(n_c)]

    def shift(value, da=0, db=0, dc=0):
        pairs = [(at(a, b, c), at(a + da, b + db, c + dc)) for a, b, c in spots]
        return lax.ppermute(value, "row", pairs)

    def shift_col(value, d):
        return lax.ppermute(value, "col", [(j, (j + d) % n_col) for j in range(n_col)])

    row_index = lax.axis_index("row").astype(jnp.int32)
    col_index = lax.axis_index("col").astype(jnp.int32)
    my_c, my_b, my_a = row_index % n_c, row_index // n_c % n_b, row_index // (n_c * n_b)

    def piece(da, db, dc):
        return (dc * n_b + db) * n_a + da

    owner = block_cols // per_piece
    owner_c, owner_b, owner_a = owner % n_c, owner // n_c % n_b, owner // (n_c * n_b)
    place_cols = (
        piece((my_a - owner_a + n_a) % n_a, (my_b - owner_b + n_b) % n_b, (my_c - owner_c + n_c) % n_c) * per_piece
        + block_cols % per_piece
    )
    place_rows = (col_index - block_rows // per_piece + n_col) % n_col * per_piece + block_rows % per_piece
    live = jnp.arange(block_rows.shape[0], dtype=jnp.int32) < block_counts[0]
    put_cols = jnp.where(live, place_cols, n_row * per_piece)
    put_rows = jnp.where(live, place_rows, n_col * per_piece)

    order = list(range(1, n_a)) + [0]
    halves = [order[:-1], order[-1:]] if n_a > 1 else [order]
    mirror_outputs = [[piece(a, b, c) for b in range(n_b) for a in order] for c in range(n_c)]
    forward_outputs = [[j] for j in range(n_col)]
    mirror_inputs = [[j] for j in range(n_col)]
    chip = [[(0, b) for b in range(n_b)] + [(a, 0) for a in range(1, n_a)]]
    rest_of_chip = [(a, b) for b in range(1, n_b) for a in range(1, n_a) if a != n_a // 2]
    rest_of_chip += [(n_a // 2, b) for b in range(1, n_b) if n_a > 1]
    if rest_of_chip:
        chip.append(rest_of_chip)
    forward_inputs = [[piece(a, b, c) for a, b in part] for c in range(n_c) for part in chip]

    def apply_operator(narrow):
        by_col = [narrow] + [shift_col(narrow, j) for j in range(1, n_col)]
        near = [narrow] + [shift(narrow, db=b) for b in range(1, n_b)]
        far = [shift(narrow, da=a) for a in range(1, n_a)]
        mirrors = block_product(
            0, mirror_inputs, mirror_outputs, [jnp.bfloat16] * len(mirror_outputs), n_row,
            block_counts, place_rows, put_cols, by_col, block_values,
        )
        mirrors = list(mirrors)
        far, mirrors[0] = lax.optimization_barrier((far, mirrors[0]))
        middle = n_a // 2
        across = [shift(far[middle - 1], db=b) for b in range(1, n_b)] if middle else []

        shares = mirrors[0].astype(jnp.float32)
        for c in range(1, n_c):
            shares += shift(mirrors[c], dc=-c).astype(jnp.float32)
        parts = []
        for b in range(n_b):
            first = b * n_a
            for half in halves:
                parts.append(shares[first : first + len(half)])
                first += len(half)
        kept = parts[: len(halves)]
        sends = [part.astype(jnp.bfloat16) for part in parts[len(halves) :]]
        firsts = [shift(send, db=-(b + 1)) for b, send in enumerate(sends[:: len(halves)])]
        far_b = [shift(part, da=a) for part in near[1:] for a in range(1, n_a) if a != middle]
        last = sends[1 :: len(halves)]
        far_b, across, firsts, last = lax.optimization_barrier((far_b, across, firsts, last))
        rest = [shift(send, db=-(b + 1)) for b, send in enumerate(last)]
        early = jnp.stack(near + far)
        by_row = [[early] + [shift(early, dc=c) for c in range(1, n_c)]]
        if far_b + across:
            late = jnp.stack(far_b + across)
            by_row.append([late] + [shift(late, dc=c) for c in range(1, n_c)])
        by_row = [part[c] for c in range(n_c) for part in by_row]

        own = []
        back = []

        def add_up(share, received, half):
            for other in received:
                share += other.astype(jnp.float32)
            for n, a in enumerate(half):
                if a:
                    back.append(shift(share[n].astype(jnp.bfloat16), da=-a))
                else:
                    own.append(share[n])

        add_up(kept[0], firsts, halves[0])
        forwards = block_product(
            1, forward_inputs, forward_outputs, [jnp.float32] + [jnp.bfloat16] * (n_col - 1), n_col,
            block_counts, place_cols, put_rows, by_row, block_values,
        )
        rest, back[:], mine = lax.optimization_barrier((rest, back, forwards[0]))
        sent = len(back)
        if len(halves) > 1:
            add_up(kept[1], rest, halves[1])
        crossed = [shift_col(forwards[j][0], -j) for j in range(1, n_col)]
        crossed, back[:sent] = lax.optimization_barrier((crossed, back[:sent]))
        forward_sum = mine[0]
        for other in crossed:
            forward_sum += other.astype(jnp.float32)
        mirror_sum = sum(own)
        for other in back:
            mirror_sum += other.astype(jnp.float32)
        return forward_sum + mirror_sum

    current = (apply_operator(vectors.astype(jnp.bfloat16)) - center_value * vectors) / radius_value
    return 2.0 * (apply_operator(current.astype(jnp.bfloat16)) - center_value * current) / radius_value - vectors


def solution(mesh):
    return jax.shard_map(
        functools.partial(shards, mesh.shape["row"], mesh.shape["col"]),
        mesh=mesh,
        in_specs=(
            P(None, ("row", "col")),
            P(("row", "col"), None, None),
            P(("row", "col")),
            P(("row", "col")),
            P(("row", "col")),
            P(),
            P(),
        ),
        out_specs=P(None, ("row", "col")),
        check_vma=False,
    )
```

```python
import functools

import jax
import jax.numpy as jnp
from jax import lax
from jax.experimental import pallas as pl
from jax.experimental.pallas import tpu as pltpu
from jax.sharding import PartitionSpec as P

CHUNK = 32
UNROLL = 64


def product_kernel(contract, inputs, outputs, count_ref, take_ref, put_ref, *refs):
    n_in = len(inputs)
    pieces = refs[:n_in]
    blocks = refs[n_in]
    outs = refs[n_in + 1 : n_in + 1 + len(outputs)]
    held, held_blocks, total, block_sems = refs[n_in + 1 + len(outputs) :]
    capacity, size_block = blocks.shape[0], blocks.shape[1]
    per_piece = held.shape[2] // size_block
    chunks = capacity // CHUNK
    count = count_ref[0]

    def block_copy(g):
        part = pl.ds(g * CHUNK, CHUNK)
        return pltpu.make_async_copy(blocks.at[part], held_blocks.at[part], block_sems.at[g])

    for g in range(chunks):
        @pl.when(g * CHUNK // UNROLL * UNROLL < count)
        def _(g=g):
            block_copy(g).start()

    total[...] = jnp.zeros_like(total)
    for part, held_pieces in zip(pieces, inputs):
        for n, p in enumerate(held_pieces):
            held[p] = part[n]

    def place(index):
        column = pl.multiple_of((index % per_piece) * size_block, size_block)
        return index // per_piece, slice(None), pl.ds(column, size_block)

    def group(first):
        products = []
        for n in range(0, UNROLL, 2):
            slot = first + n
            picked = jnp.concatenate([held[place(take_ref[slot])], held[place(take_ref[slot + 1])]], axis=0)
            if contract == 0:
                pair = jnp.concatenate([held_blocks[slot], held_blocks[slot + 1]], axis=1)
            else:
                pair = held_blocks[pl.ds(slot, 2)].reshape(2 * size_block, size_block)
            product = lax.dot_general(
                picked, pair, (((1,), (contract,)), ((), ())), preferred_element_type=jnp.float32
            )
            rows = product.shape[0] // 2
            products += [product[:rows, :size_block], product[rows:, size_block:]]
        for n, product in enumerate(products):
            total[place(put_ref[first + n])] += product

    @pl.loop(0, (count + UNROLL - 1) // UNROLL)
    def _(g):
        for n in range(UNROLL // CHUNK):
            block_copy(g * (UNROLL // CHUNK) + n).wait()
        group(g * UNROLL)

    for out, held_pieces in zip(outs, outputs):
        for n, p in enumerate(held_pieces):
            out[n] = total[p].astype(out.dtype)


def block_product(contract, inputs, outputs, dtypes, n_put, count, take, put, pieces, blocks):
    capacity, size_block = blocks.shape[0], blocks.shape[1]
    vector_count, own_rows = pieces[0].shape[-2:]
    pieces = [part.reshape(-1, vector_count, own_rows) for part in pieces]
    n_in = sum(part.shape[0] for part in pieces)
    smem = pl.BlockSpec(memory_space=pltpu.SMEM)
    vmem = pl.BlockSpec(memory_space=pltpu.VMEM)
    hbm = pl.BlockSpec(memory_space=pltpu.HBM)
    return pl.pallas_call(
        functools.partial(product_kernel, contract, inputs, outputs),
        out_shape=[
            jax.ShapeDtypeStruct((len(held), vector_count, own_rows), dtype) for held, dtype in zip(outputs, dtypes)
        ],
        in_specs=[smem] * 3 + [vmem] * len(pieces) + [hbm],
        out_specs=[pl.BlockSpec(memory_space=pltpu.VMEM)] * len(outputs),
        scratch_shapes=[
            pltpu.VMEM((n_in, vector_count, own_rows), jnp.bfloat16),
            pltpu.VMEM(blocks.shape, blocks.dtype),
            pltpu.VMEM((n_put + 1, vector_count, own_rows), jnp.float32),
            pltpu.SemaphoreType.DMA((capacity // CHUNK,)),
        ],
        compiler_params=pltpu.CompilerParams(vmem_limit_bytes=40 * 1024 * 1024),
        cost_estimate=pl.CostEstimate(
            flops=size_block,
            bytes_accessed=size_block,
            transcendentals=0,
        ),
        name="mirror" if contract == 0 else "forward",
    )(count, take, put, *pieces, pltpu.with_memory_space_constraint(blocks, pltpu.HBM))


def shards(n_row, n_col, vectors, block_values, block_rows, block_cols, block_counts, center, radius):
    size_block = block_values.shape[1]
    own_rows = vectors.shape[1]
    per_piece = own_rows // size_block
    center_value = center[0]
    radius_value = radius[0]

    n_c = 2 if n_row % 2 == 0 else 1
    n_a = 4 if (n_row // n_c) % 4 == 0 else n_row // n_c
    n_b = n_row // n_c // n_a

    def at(a, b, c):
        return ((a % n_a) * n_b + b % n_b) * n_c + c % n_c

    spots = [(a, b, c) for a in range(n_a) for b in range(n_b) for c in range(n_c)]

    def shift(value, da=0, db=0, dc=0):
        pairs = [(at(a, b, c), at(a + da, b + db, c + dc)) for a, b, c in spots]
        return lax.ppermute(value, "row", pairs)

    def shift_col(value, d):
        return lax.ppermute(value, "col", [(j, (j + d) % n_col) for j in range(n_col)])

    row_index = lax.axis_index("row").astype(jnp.int32)
    col_index = lax.axis_index("col").astype(jnp.int32)
    my_c, my_b, my_a = row_index % n_c, row_index // n_c % n_b, row_index // (n_c * n_b)

    def piece(da, db, dc):
        return (dc * n_b + db) * n_a + da

    owner = block_cols // per_piece
    owner_c, owner_b, owner_a = owner % n_c, owner // n_c % n_b, owner // (n_c * n_b)
    place_cols = (
        piece((my_a - owner_a + n_a) % n_a, (my_b - owner_b + n_b) % n_b, (my_c - owner_c + n_c) % n_c) * per_piece
        + block_cols % per_piece
    )
    place_rows = (col_index - block_rows // per_piece + n_col) % n_col * per_piece + block_rows % per_piece
    live = jnp.arange(block_rows.shape[0], dtype=jnp.int32) < block_counts[0]
    put_cols = jnp.where(live, place_cols, n_row * per_piece)
    put_rows = jnp.where(live, place_rows, n_col * per_piece)

    order = list(range(1, n_a)) + [0]
    halves = [order[:-1], order[-1:]] if n_a > 1 else [order]
    mirror_outputs = [[piece(a, b, c) for b in range(n_b) for a in order] for c in range(n_c)]
    forward_outputs = [[j] for j in range(n_col)]
    mirror_inputs = [[j] for j in range(n_col)]
    chip = [[(0, b) for b in range(n_b)] + [(a, 0) for a in range(1, n_a)]]
    rest_of_chip = [(a, b) for b in range(1, n_b) for a in range(1, n_a) if a != n_a // 2]
    rest_of_chip += [(n_a // 2, b) for b in range(1, n_b) if n_a > 1]
    if rest_of_chip:
        chip.append(rest_of_chip)
    forward_inputs = [[piece(a, b, c) for a, b in part] for c in range(n_c) for part in chip]

    def apply_operator(narrow):
        by_col = [narrow] + [shift_col(narrow, j) for j in range(1, n_col)]
        far = [shift(narrow, da=a) for a in range(1, n_a)]
        mirrors = block_product(
            0, mirror_inputs, mirror_outputs, [jnp.bfloat16] * len(mirror_outputs), n_row,
            block_counts, place_rows, put_cols, by_col, block_values,
        )
        mirrors = list(mirrors)
        far, mirrors[0], held = lax.optimization_barrier((far, mirrors[0], narrow))
        near = [held] + [shift(held, db=b) for b in range(1, n_b)]
        middle = n_a // 2
        across = [shift(far[middle - 1], db=b) for b in range(1, n_b)] if middle else []

        shares = mirrors[0].astype(jnp.float32)
        for c in range(1, n_c):
            shares += shift(mirrors[c], dc=-c).astype(jnp.float32)
        parts = []
        for b in range(n_b):
            first = b * n_a
            for half in halves:
                parts.append(shares[first : first + len(half)])
                first += len(half)
        kept = parts[: len(halves)]
        sends = [part.astype(jnp.bfloat16) for part in parts[len(halves) :]]
        firsts = [shift(send, db=-(b + 1)) for b, send in enumerate(sends[:: len(halves)])]
        far_b = [shift(part, da=a) for part in near[1:] for a in range(1, n_a) if a != middle]
        last = sends[1 :: len(halves)]
        far_b, across, firsts, last = lax.optimization_barrier((far_b, across, firsts, last))
        rest = [shift(send, db=-(b + 1)) for b, send in enumerate(last)]
        early = jnp.stack(near + far)
        by_row = [[early] + [shift(early, dc=c) for c in range(1, n_c)]]
        if far_b + across:
            late = jnp.stack(far_b + across)
            by_row.append([late] + [shift(late, dc=c) for c in range(1, n_c)])
        by_row = [part[c] for c in range(n_c) for part in by_row]

        own = []
        back = []

        def add_up(share, received, half):
            for other in received:
                share += other.astype(jnp.float32)
            for n, a in enumerate(half):
                if a:
                    back.append(shift(share[n].astype(jnp.bfloat16), da=-a))
                else:
                    own.append(share[n])

        add_up(kept[0], firsts, halves[0])
        forwards = block_product(
            1, forward_inputs, forward_outputs, [jnp.float32] + [jnp.bfloat16] * (n_col - 1), n_col,
            block_counts, place_cols, put_rows, by_row, block_values,
        )
        rest, back[:], mine = lax.optimization_barrier((rest, back, forwards[0]))
        sent = len(back)
        if len(halves) > 1:
            add_up(kept[1], rest, halves[1])
        crossed = [shift_col(forwards[j][0], -j) for j in range(1, n_col)]
        crossed, back[:sent] = lax.optimization_barrier((crossed, back[:sent]))
        forward_sum = mine[0]
        for other in crossed:
            forward_sum += other.astype(jnp.float32)
        mirror_sum = sum(own)
        for other in back:
            mirror_sum += other.astype(jnp.float32)
        return forward_sum + mirror_sum

    current = (apply_operator(vectors.astype(jnp.bfloat16)) - center_value * vectors) / radius_value
    return 2.0 * (apply_operator(current.astype(jnp.bfloat16)) - center_value * current) / radius_value - vectors


def solution(mesh):
    return jax.shard_map(
        functools.partial(shards, mesh.shape["row"], mesh.shape["col"]),
        mesh=mesh,
        in_specs=(
            P(None, ("row", "col")),
            P(("row", "col"), None, None),
            P(("row", "col")),
            P(("row", "col")),
            P(("row", "col")),
            P(),
            P(),
        ),
        out_specs=P(None, ("row", "col")),
        check_vma=False,
    )
```

```python
import functools

import jax
import jax.numpy as jnp
from jax import lax
from jax.experimental import pallas as pl
from jax.experimental.pallas import tpu as pltpu
from jax.sharding import PartitionSpec as P

CHUNK = 32
UNROLL = 64


def product_kernel(contract, inputs, outputs, count_ref, take_ref, put_ref, *refs):
    n_in = len(inputs)
    pieces = refs[:n_in]
    blocks = refs[n_in]
    outs = refs[n_in + 1 : n_in + 1 + len(outputs)]
    held, held_blocks, total, block_sems = refs[n_in + 1 + len(outputs) :]
    capacity, size_block = blocks.shape[0], blocks.shape[1]
    per_piece = held.shape[2] // size_block
    chunks = capacity // CHUNK
    count = count_ref[0]

    def block_copy(g):
        part = pl.ds(g * CHUNK, CHUNK)
        return pltpu.make_async_copy(blocks.at[part], held_blocks.at[part], block_sems.at[g])

    for g in range(chunks):
        @pl.when(g * CHUNK // UNROLL * UNROLL < count)
        def _(g=g):
            block_copy(g).start()

    total[...] = jnp.zeros_like(total)
    for part, held_pieces in zip(pieces, inputs):
        for n, p in enumerate(held_pieces):
            held[p] = part[n]

    def place(index):
        column = pl.multiple_of((index % per_piece) * size_block, size_block)
        return index // per_piece, slice(None), pl.ds(column, size_block)

    def group(first):
        products = []
        for n in range(0, UNROLL, 2):
            slot = first + n
            picked = jnp.concatenate([held[place(take_ref[slot])], held[place(take_ref[slot + 1])]], axis=0)
            if contract == 0:
                pair = jnp.concatenate([held_blocks[slot], held_blocks[slot + 1]], axis=1)
            else:
                pair = held_blocks[pl.ds(slot, 2)].reshape(2 * size_block, size_block)
            product = lax.dot_general(
                picked, pair, (((1,), (contract,)), ((), ())), preferred_element_type=jnp.float32
            )
            rows = product.shape[0] // 2
            products += [product[:rows, :size_block], product[rows:, size_block:]]
        for n, product in enumerate(products):
            total[place(put_ref[first + n])] += product

    @pl.loop(0, (count + UNROLL - 1) // UNROLL)
    def _(g):
        for n in range(UNROLL // CHUNK):
            block_copy(g * (UNROLL // CHUNK) + n).wait()
        group(g * UNROLL)

    for out, held_pieces in zip(outs, outputs):
        for n, p in enumerate(held_pieces):
            out[n] = total[p].astype(out.dtype)


def block_product(contract, inputs, outputs, dtypes, n_put, count, take, put, pieces, blocks):
    capacity, size_block = blocks.shape[0], blocks.shape[1]
    vector_count, own_rows = pieces[0].shape[-2:]
    pieces = [part.reshape(-1, vector_count, own_rows) for part in pieces]
    n_in = sum(part.shape[0] for part in pieces)
    smem = pl.BlockSpec(memory_space=pltpu.SMEM)
    vmem = pl.BlockSpec(memory_space=pltpu.VMEM)
    hbm = pl.BlockSpec(memory_space=pltpu.HBM)
    return pl.pallas_call(
        functools.partial(product_kernel, contract, inputs, outputs),
        out_shape=[
            jax.ShapeDtypeStruct((len(held), vector_count, own_rows), dtype) for held, dtype in zip(outputs, dtypes)
        ],
        in_specs=[smem] * 3 + [vmem] * len(pieces) + [hbm],
        out_specs=[pl.BlockSpec(memory_space=pltpu.VMEM)] * len(outputs),
        scratch_shapes=[
            pltpu.VMEM((n_in, vector_count, own_rows), jnp.bfloat16),
            pltpu.VMEM(blocks.shape, blocks.dtype),
            pltpu.VMEM((n_put + 1, vector_count, own_rows), jnp.float32),
            pltpu.SemaphoreType.DMA((capacity // CHUNK,)),
        ],
        compiler_params=pltpu.CompilerParams(vmem_limit_bytes=40 * 1024 * 1024),
        cost_estimate=pl.CostEstimate(
            flops=size_block,
            bytes_accessed=size_block,
            transcendentals=0,
        ),
        name="mirror" if contract == 0 else "forward",
    )(count, take, put, *pieces, pltpu.with_memory_space_constraint(blocks, pltpu.HBM))


def shards(n_row, n_col, vectors, block_values, block_rows, block_cols, block_counts, center, radius):
    size_block = block_values.shape[1]
    own_rows = vectors.shape[1]
    per_piece = own_rows // size_block
    center_value = center[0]
    radius_value = radius[0]

    n_c = 2 if n_row % 2 == 0 else 1
    n_a = 4 if (n_row // n_c) % 4 == 0 else n_row // n_c
    n_b = n_row // n_c // n_a

    def at(a, b, c):
        return ((a % n_a) * n_b + b % n_b) * n_c + c % n_c

    spots = [(a, b, c) for a in range(n_a) for b in range(n_b) for c in range(n_c)]

    def shift(value, da=0, db=0, dc=0):
        pairs = [(at(a, b, c), at(a + da, b + db, c + dc)) for a, b, c in spots]
        return lax.ppermute(value, "row", pairs)

    def shift_col(value, d):
        return lax.ppermute(value, "col", [(j, (j + d) % n_col) for j in range(n_col)])

    row_index = lax.axis_index("row").astype(jnp.int32)
    col_index = lax.axis_index("col").astype(jnp.int32)
    my_c, my_b, my_a = row_index % n_c, row_index // n_c % n_b, row_index // (n_c * n_b)

    def piece(da, db, dc):
        return (dc * n_b + db) * n_a + da

    owner = block_cols // per_piece
    owner_c, owner_b, owner_a = owner % n_c, owner // n_c % n_b, owner // (n_c * n_b)
    place_cols = (
        piece((my_a - owner_a + n_a) % n_a, (my_b - owner_b + n_b) % n_b, (my_c - owner_c + n_c) % n_c) * per_piece
        + block_cols % per_piece
    )
    place_rows = (col_index - block_rows // per_piece + n_col) % n_col * per_piece + block_rows % per_piece
    live = jnp.arange(block_rows.shape[0], dtype=jnp.int32) < block_counts[0]
    put_cols = jnp.where(live, place_cols, n_row * per_piece)
    put_rows = jnp.where(live, place_rows, n_col * per_piece)

    order = list(range(1, n_a)) + [0]
    halves = [order[:-1], order[-1:]] if n_a > 1 else [order]
    mirror_outputs = [[piece(a, b, c) for b in range(n_b) for a in order] for c in range(n_c)]
    forward_outputs = [[j] for j in range(n_col)]
    mirror_inputs = [[j] for j in range(n_col)]
    chip = [[(0, b) for b in range(n_b)] + [(a, 0) for a in range(1, n_a)]]
    rest_of_chip = [(a, b) for b in range(1, n_b) for a in range(1, n_a) if a != n_a // 2]
    rest_of_chip += [(n_a // 2, b) for b in range(1, n_b) if n_a > 1]
    chip += [[spot] for spot in rest_of_chip]
    forward_inputs = [[piece(a, b, c) for a, b in part] for c in range(n_c) for part in chip]

    def apply_operator(narrow):
        by_col = [narrow] + [shift_col(narrow, j) for j in range(1, n_col)]
        near = [narrow] + [shift(narrow, db=b) for b in range(1, n_b)]
        far = [shift(narrow, da=a) for a in range(1, n_a)]
        mirrors = block_product(
            0, mirror_inputs, mirror_outputs, [jnp.bfloat16] * len(mirror_outputs), n_row,
            block_counts, place_rows, put_cols, by_col, block_values,
        )
        mirrors = list(mirrors)
        far, mirrors[0] = lax.optimization_barrier((far, mirrors[0]))
        middle = n_a // 2
        across = [shift(far[middle - 1], db=b) for b in range(1, n_b)] if middle else []

        shares = mirrors[0].astype(jnp.float32)
        for c in range(1, n_c):
            shares += shift(mirrors[c], dc=-c).astype(jnp.float32)
        parts = []
        for b in range(n_b):
            first = b * n_a
            for half in halves:
                parts.append(shares[first : first + len(half)])
                first += len(half)
        kept = parts[: len(halves)]
        sends = [part.astype(jnp.bfloat16) for part in parts[len(halves) :]]
        firsts = [shift(send, db=-(b + 1)) for b, send in enumerate(sends[:: len(halves)])]
        far_b = [shift(part, da=a) for part in near[1:] for a in range(1, n_a) if a != middle]
        last = sends[1 :: len(halves)]
        far_b, across, firsts, last = lax.optimization_barrier((far_b, across, firsts, last))
        rest = [shift(send, db=-(b + 1)) for b, send in enumerate(last)]
        early = jnp.stack(near + far)
        by_row = [[early] + [shift(early, dc=c) for c in range(1, n_c)]]
        by_row += [[part] + [shift(part, dc=c) for c in range(1, n_c)] for part in far_b + across]
        by_row = [part[c] for c in range(n_c) for part in by_row]

        own = []
        back = []

        def add_up(share, received, half):
            for other in received:
                share += other.astype(jnp.float32)
            for n, a in enumerate(half):
                if a:
                    back.append(shift(share[n].astype(jnp.bfloat16), da=-a))
                else:
                    own.append(share[n])

        add_up(kept[0], firsts, halves[0])
        forwards = block_product(
            1, forward_inputs, forward_outputs, [jnp.float32] + [jnp.bfloat16] * (n_col - 1), n_col,
            block_counts, place_cols, put_rows, by_row, block_values,
        )
        rest, back[:], mine = lax.optimization_barrier((rest, back, forwards[0]))
        sent = len(back)
        if len(halves) > 1:
            add_up(kept[1], rest, halves[1])
        crossed = [shift_col(forwards[j][0], -j) for j in range(1, n_col)]
        crossed, back[:sent] = lax.optimization_barrier((crossed, back[:sent]))
        forward_sum = mine[0]
        for other in crossed:
            forward_sum += other.astype(jnp.float32)
        mirror_sum = sum(own)
        for other in back:
            mirror_sum += other.astype(jnp.float32)
        return forward_sum + mirror_sum

    current = (apply_operator(vectors.astype(jnp.bfloat16)) - center_value * vectors) / radius_value
    return 2.0 * (apply_operator(current.astype(jnp.bfloat16)) - center_value * current) / radius_value - vectors


def solution(mesh):
    return jax.shard_map(
        functools.partial(shards, mesh.shape["row"], mesh.shape["col"]),
        mesh=mesh,
        in_specs=(
            P(None, ("row", "col")),
            P(("row", "col"), None, None),
            P(("row", "col")),
            P(("row", "col")),
            P(("row", "col")),
            P(),
            P(),
        ),
        out_specs=P(None, ("row", "col")),
        check_vma=False,
    )
```
